32 devices in a mesh: member: 2 (over y), lat: 8 (over z, core), lon: 2 (over x), lev: 1.
Axes of the slice: x: 2, y: 2, z: 4, core: 2. Of those that a mesh axis runs over, the one named last changes fastest.
Arguments:
- adjoint: float32 [6, 32, 64, 3072], P('member', 'lev', 'lat', 'lon'), parts along dimension 0, may hold values from -6 to 6
- depth: bfloat16 [32, 64, 3072], P('lev', 'lat', 'lon'), may hold values from 0.5 to 2
- zonal_coef: float32 [64], replicated, may hold values from 0.05 to 0.5
- merid_coef: float32 [64], replicated, may hold values from 0.05 to 0.5
- coriolis: float32 [64], replicated, may hold values from -0.5 to 0.5
- layer_weight: float32 [32], P('lev'), may hold values from 0.02 to 0.2
- cutoffs: int32 [64], replicated, may hold values from 0 to 1023, as said below
- polar_flags: int32 [64], replicated, may hold values from 0 to 1, as said below
Outputs:
- adjoint_next: float32 [6, 32, 64, 3072], P('member', 'lev', 'lat', 'lon'), parts along dimension 0
The draws below stay inside these ranges and needn't reach their ends.
There are 2 independent parts, one for each index of `member`. The reference program is written for one: setup_inputs(seed, part) draws one part's arguments, and reference() takes and returns one part's arrays. A program takes and returns all parts, laid end to end along the dimension named above; an argument that names none is the same for every part. Nothing has to cross between parts.
Inputs may be any that keep to these rules, and one draw needn't show every extreme that they name: cutoffs[0] is 1023 and cutoffs[63] is 0. `polar_flags`: the flagged rows form one run that starts at row 0 and one that ends at row 63; each run has 12 to 24 rows, and one of the two has exactly 24.
All inputs are finite; a program needn't handle non-finite values.
Results may differ from the reference program's by a relative error of at most 0.0003.
Values sent between devices are 32-bit elements; how exact they have to be, the bound alone decides.
A program may use at most 128 MiB of HBM per device.

```python
import math
import jax
import jax.numpy as jnp

NLON = 3072
KMAX = 1024
LEVELS = 32
NLAT = 64
POLE_ROWS = 24


def polar_runs(key):
    folded = jax.random.fold_in(key, 11)
    first_key, second_key = jax.random.split(folded)
    shorter = jax.random.randint(first_key, (), POLE_ROWS // 2, POLE_ROWS + 1)
    north_full = jax.random.randint(second_key, (), 0, 2)
    north_count = jnp.where(north_full == 0, POLE_ROWS, shorter)
    south_count = jnp.where(north_full == 0, shorter, POLE_ROWS)
    row_index = jnp.arange(NLAT, dtype=jnp.int32)
    flag_rows = jnp.logical_or(row_index < north_count, row_index >= NLAT - south_count)
    return flag_rows.astype(jnp.int32)


def draw_polar_flags(key, part):
    return polar_runs(key)


def draw_cutoffs(key, part):
    folded = jax.random.fold_in(key, 23)
    cut_rows = jax.random.randint(folded, (NLAT,), 0, KMAX)
    cut_rows = cut_rows.at[0].set(KMAX - 1)
    cut_rows = cut_rows.at[NLAT - 1].set(0)
    return cut_rows.astype(jnp.int32)


def steps_of(own_key, dims, pieces, low, high):
    loudness = 1.0
    for position, shards_of in pieces:
        steps = jax.random.uniform(jax.random.fold_in(jax.random.fold_in(own_key, 6), position), (shards_of,), jnp.float32, low / len(pieces), high / len(pieces))
        loudness = loudness * jnp.repeat(jnp.exp(steps), dims[position] // shards_of).reshape((-1,) + (1,) * (len(dims) - 1 - position))
    return loudness


def normal_values(key, extent, spread, limit, pieces=(), kind=jnp.bfloat16):
    values = spread * jax.random.normal(key, extent, jnp.float32)
    if pieces:
        values = values * steps_of(key, extent, pieces, -0.22, 0.18)
    return jnp.clip(values, -limit, limit).astype(kind)


def setup_inputs(seed: int = 0, part: int = 0) -> dict:
    keys = jax.random.split(jax.random.key(seed), 9)
    own_keys = jax.random.split(jax.random.fold_in(keys[8], part), 9)
    adjoint = normal_values(own_keys[0], (3, LEVELS, NLAT, NLON), 1.0, 6.0, ((2, 8), (3, 2)), jnp.float32)
    depth = jnp.clip(0.5 + 1.5 * jax.random.uniform(keys[1], (LEVELS, NLAT, NLON), jnp.float32) ** steps_of(keys[1], (LEVELS, NLAT, NLON), ((1, 8), (2, 2)), -0.2, 0.2), 0.5, 2.0).astype(jnp.bfloat16)
    zonal_coef = jnp.clip(jnp.exp(jax.random.uniform(keys[2], (NLAT,), jnp.float32, math.log(0.05), math.log(0.5))), 0.05, 0.5)
    merid_coef = jnp.clip(jnp.exp(jax.random.uniform(keys[3], (NLAT,), jnp.float32, math.log(0.05), math.log(0.5))), 0.05, 0.5)
    coriolis = jnp.clip(jax.random.uniform(keys[4], (NLAT,), jnp.float32, -0.5, 0.5), -0.5, 0.5)
    layer_weight = jnp.clip(jnp.exp(jax.random.uniform(keys[5], (LEVELS,), jnp.float32, math.log(0.02), math.log(0.2))), 0.02, 0.2)
    cutoffs = draw_cutoffs(jax.random.fold_in(keys[8], 71), part)
    polar_flags = draw_polar_flags(jax.random.fold_in(keys[8], 71), part)
    return dict(adjoint=adjoint, depth=depth, zonal_coef=zonal_coef, merid_coef=merid_coef, coriolis=coriolis, layer_weight=layer_weight, cutoffs=cutoffs, polar_flags=polar_flags)


def zonal_adjoint(field, zonal_rows):
    return zonal_rows * (jnp.roll(field, 1, axis=-1) - jnp.roll(field, -1, axis=-1))


def merid_adjoint(field, merid_rows):
    scaled = merid_rows * field
    padded = jnp.pad(scaled, ((0, 0), (1, 1), (0, 0)))
    return padded[:, :-2] - padded[:, 2:]


def reference(adjoint, depth, zonal_coef, merid_coef, coriolis, layer_weight, cutoffs, polar_flags):
    spectrum = jnp.fft.rfft(adjoint, axis=-1)
    wave_index = jnp.arange(NLON // 2 + 1, dtype=jnp.int32)
    kept_modes = (wave_index[None, :] <= cutoffs[:, None]).astype(jnp.float32)
    smoothed = jnp.fft.irfft(spectrum * kept_modes[None, None, :, :], n=NLON, axis=-1).astype(jnp.float32)
    filtered = jnp.where(polar_flags[None, None, :, None] > 0, smoothed, adjoint)
    q_height = filtered[0]
    q_east = filtered[1]
    q_north = filtered[2]
    zonal_rows = zonal_coef[None, :, None]
    merid_rows = merid_coef[None, :, None]
    coriolis_rows = coriolis[None, :, None]
    height_flux = depth.astype(jnp.float32) * q_height
    column_force = -zonal_adjoint(q_east, zonal_rows) - merid_adjoint(q_north, merid_rows)
    column_sum = jnp.cumsum(column_force, axis=0)
    new_height = adjoint[0] + layer_weight[:, None, None] * column_sum
    new_east = adjoint[1] - zonal_adjoint(height_flux, zonal_rows) - coriolis_rows * q_north
    new_north = adjoint[2] - merid_adjoint(height_flux, merid_rows) + coriolis_rows * q_east
    return jnp.stack([new_height, new_east, new_north])
```

```python
import functools
import math

import jax
import jax.numpy as jnp
import ml_dtypes
import numpy as np
from jax import lax
from jax.experimental import pallas as pl
from jax.experimental.pallas import tpu as pltpu
from jax.sharding import PartitionSpec as P

KMAX = 1024
POLE_ROWS = 24


def extended(cells, sides, width, closed):
    for axis, dim in sides:
        count = lax.axis_size(axis)
        ends = count if closed else count - 1
        head = lax.slice_in_dim(cells, 0, width, axis=dim)
        tail = lax.slice_in_dim(cells, cells.shape[dim] - width, cells.shape[dim], axis=dim)
        cells = jnp.concatenate(
            [
                lax.ppermute(tail, axis, [(i, (i + 1) % count) for i in range(ends)]),
                cells,
                lax.ppermute(head, axis, [((i + 1) % count, i) for i in range(ends)]),
            ],
            axis=dim,
        )
    return cells


def entering(value, axis, join, neutral):
    count, mine = (lax.axis_size(axis), lax.axis_index(axis))
    pieces = lax.all_gather(value, axis)
    total = jnp.full_like(value, 0) + jnp.asarray(neutral, value.dtype)

    def turn(position, total):
        longer = join(total, pieces[position])
        return jnp.where(position < mine, longer, total)

    return lax.fori_loop(0, count - 1, turn, total)


def wave_table(col_count, wave_start, wave_count, circle):
    columns = lax.iota(jnp.int32, col_count)
    wave_index = wave_start + lax.iota(jnp.int32, wave_count)
    phase = columns[:, None] * wave_index[None, :] % circle
    angle = phase.astype(jnp.float32) * (2.0 * math.pi / circle)
    return jnp.concatenate([jnp.cos(angle), jnp.sin(angle)], axis=1)


def keep_weights(cut_rows, wave_start, wave_count, circle):
    wave_index = wave_start + lax.iota(jnp.int32, wave_count)
    factor = jnp.where(wave_index == 0, 1.0, 2.0) / circle
    kept = (wave_index[None, :] <= cut_rows[:, None]).astype(jnp.float32) * factor[None, :]
    return jnp.concatenate([kept, kept], axis=1)


def block_width():
    return min(KMAX, 128)


def project_rows(row_data, cut_rows):
    circle = row_data.shape[1]
    width = block_width()
    result = jnp.zeros(row_data.shape, jnp.float32)
    for block_index in range(KMAX // width):
        table = wave_table(circle, block_index * width, width, circle)
        coefs = jnp.dot(
            row_data, table, precision=lax.Precision.HIGHEST, preferred_element_type=jnp.float32
        )
        weights = keep_weights(cut_rows, block_index * width, width, circle)
        result = result + jnp.dot(
            coefs * weights,
            table.T,
            precision=lax.Precision.HIGHEST,
            preferred_element_type=jnp.float32,
        )
    return result


def transpose_filter(row_data, cut_rows, flag_rows):
    lon_count = lax.axis_size("lon")
    lon_index = lax.axis_index("lon")
    share = row_data.shape[0] // lon_count
    full_rows = lax.all_to_all(row_data, "lon", split_axis=0, concat_axis=1, tiled=True)
    my_cuts = lax.dynamic_slice_in_dim(cut_rows, lon_index * share, share)
    smoothed = project_rows(full_rows, my_cuts)
    returned = lax.all_to_all(smoothed, "lon", split_axis=1, concat_axis=0, tiled=True)
    return jnp.where(flag_rows[:, None] > 0, returned, row_data)


def polar_filter(row_data, cut_rows, flag_rows):
    return transpose_filter(row_data, cut_rows, flag_rows)


def on_device(adjoint, depth, zonal_coef, merid_coef, coriolis, layer_weight, cutoffs, polar_flags):
    fields, level_count, lat_rows, lon_cells = adjoint.shape
    lat_index = lax.axis_index("lat")
    lat_total = lat_rows * lax.axis_size("lat")
    stacked = adjoint.reshape(fields * level_count, lat_rows, lon_cells)
    bands = lax.all_to_all(stacked, "lat", split_axis=0, concat_axis=1, tiled=True)
    groups = bands.shape[0]
    polar_block = jnp.concatenate([bands[:, :POLE_ROWS], bands[:, lat_total - POLE_ROWS :]], axis=1)
    polar_cuts = jnp.concatenate([cutoffs[:POLE_ROWS], cutoffs[lat_total - POLE_ROWS :]])
    polar_marks = jnp.concatenate([polar_flags[:POLE_ROWS], polar_flags[lat_total - POLE_ROWS :]])
    row_data = polar_block.reshape(groups * 2 * POLE_ROWS, lon_cells)
    cut_rows = jnp.tile(polar_cuts, groups)
    flag_rows = jnp.tile(polar_marks, groups)
    treated = polar_filter(row_data, cut_rows, flag_rows)
    treated = treated.reshape(groups, 2 * POLE_ROWS, lon_cells)
    bands = jnp.concatenate(
        [
            treated[:, :POLE_ROWS],
            bands[:, POLE_ROWS : lat_total - POLE_ROWS],
            treated[:, POLE_ROWS:],
        ],
        axis=1,
    )
    filtered = lax.all_to_all(bands, "lat", split_axis=1, concat_axis=0, tiled=True).reshape(
        adjoint.shape
    )
    q_height = filtered[0]
    q_east = filtered[1]
    q_north = filtered[2]
    zonal_rows = lax.dynamic_slice_in_dim(zonal_coef, lat_index * lat_rows, lat_rows)[None, :, None]
    merid_rows = lax.dynamic_slice_in_dim(merid_coef, lat_index * lat_rows, lat_rows)[None, :, None]
    coriolis_rows = lax.dynamic_slice_in_dim(coriolis, lat_index * lat_rows, lat_rows)[
        None, :, None
    ]
    height_flux = depth.astype(jnp.float32) * q_height
    north_pair = jnp.stack([merid_rows * q_north, merid_rows * height_flux])
    north_rims = extended(north_pair, (("lat", 2),), 1, False)
    merid_diff = north_rims[:, :, :-2] - north_rims[:, :, 2:]
    east_pair = jnp.stack([q_east, height_flux])
    east_rims = extended(east_pair, (("lon", 3),), 1, True)
    zonal_diff = zonal_rows * (east_rims[..., :-2] - east_rims[..., 2:])
    column_force = -zonal_diff[0] - merid_diff[0]
    running = jnp.cumsum(column_force, axis=0)
    carried = entering(
        jnp.sum(column_force, axis=0), "lev", jnp.add, jnp.zeros((lat_rows, lon_cells), jnp.float32)
    )
    new_height = adjoint[0] + layer_weight[:, None, None] * (running + carried[None])
    new_east = adjoint[1] - zonal_diff[1] - coriolis_rows * q_north
    new_north = adjoint[2] - merid_diff[1] + coriolis_rows * q_east
    return jnp.stack([new_height, new_east, new_north])


REMOTE = 28
OWN = 28
OTHER = 30
FAR = 32
TILE = 256
LANES = 128
ROWS = 8
ORDER = (2, 0, 1)
MESH = pl.DeviceIdType.MESH


def halves(value):
    high = value.astype(jnp.bfloat16)
    return high, (value - high.astype(jnp.float32)).astype(jnp.bfloat16)


def split_table(value):
    high = np.asarray(value, np.float32).astype(ml_dtypes.bfloat16)
    low = (np.asarray(value, np.float32) - high.astype(np.float32)).astype(ml_dtypes.bfloat16)
    return high, low


def factors(matrix, rank):
    u, s, v = np.linalg.svd(matrix, full_matrices=False)
    size = np.sqrt(s[:rank])
    return u[:, :rank] * size, v[:rank].T * size


@functools.lru_cache(maxsize=None)
def kernel_tables(cells):
    circle = 2 * cells

    def kernel(distance):
        wave = circle * np.sin(np.pi * (distance % (2 * circle)) / circle)
        return np.where(distance % circle == 0, 0.0, 1.0 / np.where(distance % circle == 0, 1.0, wave))

    n = np.arange(cells)
    here = kernel(n[:, None] - n[None, :])
    project = np.zeros((cells, LANES))
    expand = np.zeros((LANES, cells))
    left, right = factors(kernel(n[:, None] - n[None, :] - cells), REMOTE)
    project[:, :REMOTE] = right
    expand[:REMOTE] = left.T
    project[:, OWN] = kernel(cells - 1 - n)
    project[:, OWN + 1] = kernel(0 - n)
    project[:, OTHER] = kernel(cells - 1 - n - cells)
    project[:, OTHER + 1] = kernel(0 - n - cells)
    blocks = cells // TILE
    at = FAR
    for block in range(blocks):
        part = slice(block * TILE, (block + 1) * TILE)
        far = here[part].copy()
        far[:, part] = 0.0
        rank = 12 if block in (0, blocks - 1) else 18
        left, right = factors(far, rank)
        project[:, at : at + rank] = right
        expand[at : at + rank, part] = left.T
        at += rank
    near = kernel(n[:TILE, None] - n[None, :TILE]).T
    project_high, project_low = split_table(project)
    expand_high, expand_low = split_table(expand)
    near_high, near_low = split_table(near)
    return (
        np.concatenate([project_high, project_low], axis=1),
        np.concatenate([expand_high, expand_high, expand_low]),
        np.concatenate([near_high, near_high, near_low]),
    )


def column(ref, first, kind=jnp.float32):
    row = lax.broadcasted_iota(jnp.int32, (ROWS, LANES), 0)
    value = jnp.zeros((ROWS, LANES), kind)
    for turn in range(ROWS):
        value = jnp.where(row == turn, ref[first + turn], value)
    return value


def across(value, width):
    return jnp.concatenate([value] * (width // LANES), axis=1)


def filter_kernel(
    merid_ref, cuts_ref, flags_ref, x_hbm, depth_hbm, project_hbm, expand_hbm, near_hbm,
    q_hbm, rims_ref, edges_ref,
    x_ref, depth_ref, project_ref, expand_ref, near_ref, high_ref, low_ref, code_ref, edge_ref, send_ref, take_ref,
    rows_ref, brink_ref, load_sem, table_sem, store_sem, out_sem, in_sem, up_sem, up_in_sem, down_sem, down_in_sem,
):
    fields, levels, rows, cells = x_ref.shape
    circle = 2 * cells
    count = levels * rows
    half = count // 2
    lat_count = lax.axis_size("lat")
    lat = lax.axis_index("lat")
    lon = lax.axis_index("lon")
    loads = [pltpu.make_async_copy(x_hbm.at[f], x_ref.at[f], load_sem.at[f]) for f in range(fields)]
    tables = [
        pltpu.make_async_copy(source, target, table_sem.at[turn])
        for turn, (source, target) in enumerate(
            ((project_hbm, project_ref), (depth_hbm, depth_ref), (near_hbm, near_ref), (expand_hbm, expand_ref))
        )
    ]
    loads[ORDER[0]].start()
    tables[0].start()
    loads[ORDER[1]].start()
    tables[1].start()
    loads[ORDER[2]].start()
    tables[2].start()
    tables[3].start()

    barrier = pltpu.get_barrier_semaphore()
    pl.semaphore_signal(barrier, inc=1, device_id={"lon": 1 - lon}, device_id_type=MESH)

    @pl.when(lat > 0)
    def _():
        pl.semaphore_signal(barrier, inc=1, device_id={"lat": lat - 1}, device_id_type=MESH)

    @pl.when(lat < lat_count - 1)
    def _():
        pl.semaphore_signal(barrier, inc=1, device_id={"lat": lat + 1}, device_id_type=MESH)

    first = lat * rows
    cuts = column(cuts_ref, first, jnp.int32)
    on = jnp.where(column(flags_ref, first, jnp.int32) > 0, 1.0, 0.0)
    merid = column(merid_ref, first)
    kept = (2 * cuts + 1).astype(jnp.float32)
    keep = jnp.where(on > 0.0, kept * (1.0 / circle), 1.0)
    odd = jnp.bitwise_and(cuts, 1)
    sign = on * jnp.where(odd == 0, -1.0, 1.0)
    place = lax.broadcasted_iota(jnp.int32, (rows, cells), 1).astype(jnp.float32)
    phase = across(kept, cells) * place
    phase = phase - jnp.floor(phase * (1.0 / (2 * circle))) * (2.0 * circle)
    angle = phase * (math.pi / circle)
    cos = across(on, cells) * jnp.cos(angle)
    sin = across(on, cells) * jnp.sin(angle)
    lane = lax.broadcasted_iota(jnp.int32, (rows, LANES), 1)

    def at_edges(end, start, low):
        return jnp.where(lane == low, end, jnp.where(lane == low + 1, start, 0.0))

    end_cos, end_sin = cos[:, cells - 1 :], sin[:, cells - 1 :]
    start_cos, start_sin = cos[:, :1], sin[:, :1]
    mix_cos = at_edges(end_sin, start_sin, OWN) + at_edges(sign * end_cos, sign * start_cos, OTHER)
    mix_sin = at_edges(-end_cos, -start_cos, OWN) + at_edges(sign * end_sin, sign * start_sin, OTHER)
    rows_ref[0] = cos
    rows_ref[1] = sin

    def exchange(field):
        return pltpu.make_async_remote_copy(
            src_ref=send_ref.at[field], dst_ref=take_ref.at[field], send_sem=out_sem.at[field],
            recv_sem=in_sem.at[field], device_id={"lon": 1 - lon}, device_id_type=MESH,
        )

    def spread(value):
        return jnp.broadcast_to(value[None], (levels,) + value.shape).reshape(count, value.shape[1])

    def climb(which):
        return pltpu.make_async_remote_copy(
            src_ref=brink_ref.at[1, which], dst_ref=edges_ref.at[0, which], send_sem=up_sem.at[which],
            recv_sem=up_in_sem.at[which], device_id={"lat": lat + 1}, device_id_type=MESH,
        )

    def descend(which):
        return pltpu.make_async_remote_copy(
            src_ref=brink_ref.at[0, which], dst_ref=edges_ref.at[1, which], send_sem=down_sem.at[which],
            recv_sem=down_in_sem.at[which], device_id={"lat": lat - 1}, device_id_type=MESH,
        )

    lane_all = lax.broadcasted_iota(jnp.int32, (count, LANES), 1)
    part = 8
    for turn, field in enumerate(ORDER):
        loads[field].wait()
        for group in range(levels // part):
            x = x_ref[field, group * part : (group + 1) * part]
            for which in range(2):
                high, low = halves((x * rows_ref[which][None]).reshape(part * rows, cells))
                at = slice(which * count + group * part * rows, which * count + (group + 1) * part * rows)
                high_ref[field, at] = high
                low_ref[field, at] = low
        if turn == 0:
            tables[0].wait()
        table = project_ref[...]
        total = jnp.dot(high_ref[field], table, preferred_element_type=jnp.float32)
        total = total + jnp.dot(low_ref[field], table, preferred_element_type=jnp.float32)
        code = total[:, :LANES] + total[:, LANES:]
        code_ref[field] = code
        code_cos, code_sin = code[:count], code[count:]
        message = jnp.where(lane_all < 32, code_cos, pltpu.roll(code_sin, 32, 1))
        if field < 2:
            edge = spread(mix_cos) * code_cos + spread(mix_sin) * code_sin
            start, end = x_ref[field, :, :, :LANES], x_ref[field, :, :, cells - LANES :]
            start, end = start.reshape(count, LANES)[:, :1], end.reshape(count, LANES)[:, LANES - 1 :]
            edge = edge + spread(keep) * jnp.where(lane_all == OWN, end, jnp.where(lane_all == OWN + 1, start, 0.0))
            edge_ref[field] = edge
            message = jnp.where(jnp.logical_and(lane_all >= OWN, lane_all < OWN + 2), edge, message)
        if field == 0:
            tables[1].wait()
            start, end = depth_ref[:, :, :LANES], depth_ref[:, :, cells - LANES :]
            start = start.astype(jnp.float32).reshape(count, LANES)[:, :1]
            end = end.astype(jnp.float32).reshape(count, LANES)[:, LANES - 1 :]
            message = jnp.where(lane_all == OWN + 32, end, jnp.where(lane_all == OWN + 33, start, message))
        send_ref[field] = jnp.where(lane_all[:half] < 64, message[:half], pltpu.roll(message[half:], 64, 1))
        if turn == 0:
            greeted = 1 + jnp.where(lat > 0, 1, 0) + jnp.where(lat < lat_count - 1, 1, 0)
            pl.semaphore_wait(barrier, greeted)
        exchange(field).start()

    @pl.when(lat == 0)
    def _():
        edges_ref[0] = jnp.zeros(edges_ref.shape[1:], jnp.float32)

    @pl.when(lat == lat_count - 1)
    def _():
        edges_ref[1] = jnp.zeros(edges_ref.shape[1:], jnp.float32)

    tables[2].wait()
    tables[3].wait()
    stores = []
    for field in ORDER:
        exchange(field).wait_recv()
        taken = take_ref[field]
        taken = jnp.concatenate([taken, pltpu.roll(taken, 64, 1)])
        turned = pltpu.roll(taken, 96, 1)
        if field < 2:
            rims = taken + pltpu.roll(edge_ref[field], LANES - 2, 1)
            if field == 0:
                rims = rims * turned
            rims_ref[field] = rims.reshape(levels, rows, LANES)
        signs = spread(sign)
        code = code_ref[field]
        code = jnp.concatenate(
            [
                jnp.where(lane_all < REMOTE, signs * turned, code[:count]),
                jnp.where(lane_all < REMOTE, -signs * taken, code[count:]),
            ]
        )
        code_high, code_low = halves(code)
        for block in range(cells // TILE):
            at = slice(block * TILE, (block + 1) * TILE)
            high, low = high_ref[field, :, at], low_ref[field, :, at]
            terms = jnp.concatenate([high, low, high, code_high, code_low, code_high], axis=1)
            weights = jnp.concatenate([near_ref[...], expand_ref[:, at]], axis=0)
            value = jnp.dot(terms, weights, preferred_element_type=jnp.float32)
            shape = (levels, rows, TILE)
            result = across(keep, TILE)[None] * x_ref[field, :, :, at]
            result = result + rows_ref[1, :, at][None] * value[:count].reshape(shape)
            result = result - rows_ref[0, :, at][None] * value[count:].reshape(shape)
            x_ref[field, :, :, at] = result
            if field != 1:
                edge = result
                if field == 0:
                    edge = result * depth_ref[:, :, at].astype(jnp.float32)
                edge = edge * across(merid, TILE)[None]
                which = 0 if field == 2 else 1
                brink_ref[0, which, :, at] = edge[:, 0, :]
                brink_ref[1, which, :, at] = edge[:, rows - 1, :]
        store = pltpu.make_async_copy(x_ref.at[field], q_hbm.at[field], store_sem.at[field])
        store.start()
        stores.append(store)
        if field != 1:
            which = 0 if field == 2 else 1

            @pl.when(lat < lat_count - 1)
            def _():
                climb(which).start()

            @pl.when(lat > 0)
            def _():
                descend(which).start()

    for store in stores:
        store.wait()
    for field in ORDER:
        exchange(field).wait_send()

    @pl.when(lat < lat_count - 1)
    def _():
        for which in range(2):
            climb(which).wait_send()
            descend(which).wait_recv()

    @pl.when(lat > 0)
    def _():
        for which in range(2):
            descend(which).wait_send()
            climb(which).wait_recv()


def final_kernel(
    zonal_ref, merid_ref, coriolis_ref, weight_ref, x_ref, q_ref, depth_ref, edges_ref, rims_ref, out_ref, run_ref
):
    step = pl.program_id(0)
    _, levels, rows, cells = x_ref.shape
    first = lax.axis_index("lat") * rows
    zonal = across(column(zonal_ref, first), cells)
    merid = across(column(merid_ref, first), cells)
    coriolis = across(column(coriolis_ref, first), cells)
    row = lax.broadcasted_iota(jnp.int32, (rows, cells), 0)
    lane = lax.broadcasted_iota(jnp.int32, (rows, cells), 1)

    def zonal_adjoint(value, west, east):
        left = jnp.where(lane == 0, west, pltpu.roll(value, 1, 1))
        right = jnp.where(lane == cells - 1, east, pltpu.roll(value, cells - 1, 1))
        return zonal * (left - right)

    def merid_adjoint(value, before, after):
        value = merid * value
        up = jnp.where(row == 0, before, pltpu.roll(value, 1, 0))
        down = jnp.where(row == rows - 1, after, pltpu.roll(value, rows - 1, 0))
        return up - down

    @pl.when(step == 0)
    def _():
        run_ref[...] = jnp.zeros_like(run_ref)

    run = run_ref[...]
    for level in range(levels):
        height, east, north = q_ref[0, level], q_ref[1, level], q_ref[2, level]
        flux = depth_ref[level].astype(jnp.float32) * height
        line = pl.ds(level, 1)
        flux_rims, east_rims = rims_ref[0, level], rims_ref[1, level]
        run = run - (
            zonal_adjoint(east, east_rims[:, OWN : OWN + 1], east_rims[:, OWN + 1 : OWN + 2])
            + merid_adjoint(north, edges_ref[0, 0, line, :], edges_ref[1, 0, line, :])
        )
        out_ref[0, level] = x_ref[0, level] + weight_ref[step * levels + level] * run
        out_ref[1, level] = (
            x_ref[1, level]
            - zonal_adjoint(flux, flux_rims[:, OWN : OWN + 1], flux_rims[:, OWN + 1 : OWN + 2])
            - coriolis * north
        )
        out_ref[2, level] = (
            x_ref[2, level]
            - merid_adjoint(flux, edges_ref[0, 1, line, :], edges_ref[1, 1, line, :])
            + coriolis * east
        )
    run_ref[...] = run


def on_pair(adjoint, depth, zonal_coef, merid_coef, coriolis, layer_weight, cutoffs, polar_flags):
    fields, level_count, rows, cells = adjoint.shape
    project, expand, near = (jnp.asarray(table) for table in kernel_tables(cells))
    count = level_count * rows
    scalars = pl.BlockSpec(memory_space=pltpu.SMEM)
    there = pl.BlockSpec(memory_space=pl.ANY)
    close = pl.BlockSpec(memory_space=pltpu.VMEM)
    single = jnp.float32
    dma = pltpu.SemaphoreType.DMA

    q, rims, edges = pl.pallas_call(
        filter_kernel,
        in_specs=[scalars] * 3 + [there] * 5,
        out_specs=[there, close, close],
        out_shape=[
            jax.ShapeDtypeStruct(adjoint.shape, single),
            jax.ShapeDtypeStruct((2, level_count, rows, LANES), single),
            jax.ShapeDtypeStruct((2, 2, level_count, cells), single),
        ],
        scratch_shapes=[
            pltpu.VMEM(adjoint.shape, single),
            pltpu.VMEM(depth.shape, depth.dtype),
            pltpu.VMEM(project.shape, project.dtype),
            pltpu.VMEM(expand.shape, expand.dtype),
            pltpu.VMEM(near.shape, near.dtype),
            pltpu.VMEM((fields, 2 * count, cells), jnp.bfloat16),
            pltpu.VMEM((fields, 2 * count, cells), jnp.bfloat16),
            pltpu.VMEM((fields, 2 * count, LANES), single),
            pltpu.VMEM((2, count, LANES), single),
            pltpu.VMEM((fields, count // 2, LANES), single),
            pltpu.VMEM((fields, count // 2, LANES), single),
            pltpu.VMEM((2, rows, cells), single),
            pltpu.VMEM((2, 2, level_count, cells), single),
            dma((3,)),
            dma((4,)),
            dma((3,)),
            dma((3,)),
            dma((3,)),
            dma((2,)),
            dma((2,)),
            dma((2,)),
            dma((2,)),
        ],
        compiler_params=pltpu.CompilerParams(
            collective_id=0, has_side_effects=True, vmem_limit_bytes=48 * 2**20
        ),
    )(merid_coef, cutoffs, polar_flags, adjoint, depth, project, expand, near)

    part = 8
    four = pl.BlockSpec((fields, part, rows, cells), lambda i: (0, i, 0, 0))
    three = pl.BlockSpec((part, rows, cells), lambda i: (i, 0, 0))
    return pl.pallas_call(
        final_kernel,
        grid=(level_count // part,),
        in_specs=[scalars] * 4
        + [
            four,
            four,
            three,
            pl.BlockSpec((2, 2, part, cells), lambda i: (0, 0, i, 0)),
            pl.BlockSpec((2, part, rows, LANES), lambda i: (0, i, 0, 0)),
        ],
        out_specs=four,
        out_shape=jax.ShapeDtypeStruct(adjoint.shape, single),
        scratch_shapes=[pltpu.VMEM((rows, cells), single)],
        compiler_params=pltpu.CompilerParams(vmem_limit_bytes=32 * 2**20),
    )(zonal_coef, merid_coef, coriolis, layer_weight, adjoint, q, depth, edges, rims)


def plan_for(mesh):
    return on_pair if mesh.shape["lon"] == 2 and mesh.shape["lev"] == 1 else on_device


def solution(mesh):
    return jax.shard_map(
        plan_for(mesh),
        mesh=mesh,
        in_specs=(
            P("member", "lev", "lat", "lon"),
            P("lev", "lat", "lon"),
            P(),
            P(),
            P(),
            P("lev"),
            P(),
            P(),
        ),
        out_specs=P("member", "lev", "lat", "lon"),
        check_vma=False,
    )
```

```python
import functools
import math

import jax
import jax.numpy as jnp
import ml_dtypes
import numpy as np
from jax import lax
from jax.experimental import pallas as pl
from jax.experimental.pallas import tpu as pltpu
from jax.sharding import PartitionSpec as P

KMAX = 1024
POLE_ROWS = 24


def extended(cells, sides, width, closed):
    for axis, dim in sides:
        count = lax.axis_size(axis)
        ends = count if closed else count - 1
        head = lax.slice_in_dim(cells, 0, width, axis=dim)
        tail = lax.slice_in_dim(cells, cells.shape[dim] - width, cells.shape[dim], axis=dim)
        cells = jnp.concatenate(
            [
                lax.ppermute(tail, axis, [(i, (i + 1) % count) for i in range(ends)]),
                cells,
                lax.ppermute(head, axis, [((i + 1) % count, i) for i in range(ends)]),
            ],
            axis=dim,
        )
    return cells


def entering(value, axis, join, neutral):
    count, mine = (lax.axis_size(axis), lax.axis_index(axis))
    pieces = lax.all_gather(value, axis)
    total = jnp.full_like(value, 0) + jnp.asarray(neutral, value.dtype)

    def turn(position, total):
        longer = join(total, pieces[position])
        return jnp.where(position < mine, longer, total)

    return lax.fori_loop(0, count - 1, turn, total)


def wave_table(col_count, wave_start, wave_count, circle):
    columns = lax.iota(jnp.int32, col_count)
    wave_index = wave_start + lax.iota(jnp.int32, wave_count)
    phase = columns[:, None] * wave_index[None, :] % circle
    angle = phase.astype(jnp.float32) * (2.0 * math.pi / circle)
    return jnp.concatenate([jnp.cos(angle), jnp.sin(angle)], axis=1)


def keep_weights(cut_rows, wave_start, wave_count, circle):
    wave_index = wave_start + lax.iota(jnp.int32, wave_count)
    factor = jnp.where(wave_index == 0, 1.0, 2.0) / circle
    kept = (wave_index[None, :] <= cut_rows[:, None]).astype(jnp.float32) * factor[None, :]
    return jnp.concatenate([kept, kept], axis=1)


def block_width():
    return min(KMAX, 128)


def project_rows(row_data, cut_rows):
    circle = row_data.shape[1]
    width = block_width()
    result = jnp.zeros(row_data.shape, jnp.float32)
    for block_index in range(KMAX // width):
        table = wave_table(circle, block_index * width, width, circle)
        coefs = jnp.dot(
            row_data, table, precision=lax.Precision.HIGHEST, preferred_element_type=jnp.float32
        )
        weights = keep_weights(cut_rows, block_index * width, width, circle)
        result = result + jnp.dot(
            coefs * weights,
            table.T,
            precision=lax.Precision.HIGHEST,
            preferred_element_type=jnp.float32,
        )
    return result


def transpose_filter(row_data, cut_rows, flag_rows):
    lon_count = lax.axis_size("lon")
    lon_index = lax.axis_index("lon")
    share = row_data.shape[0] // lon_count
    full_rows = lax.all_to_all(row_data, "lon", split_axis=0, concat_axis=1, tiled=True)
    my_cuts = lax.dynamic_slice_in_dim(cut_rows, lon_index * share, share)
    smoothed = project_rows(full_rows, my_cuts)
    returned = lax.all_to_all(smoothed, "lon", split_axis=1, concat_axis=0, tiled=True)
    return jnp.where(flag_rows[:, None] > 0, returned, row_data)


def polar_filter(row_data, cut_rows, flag_rows):
    return transpose_filter(row_data, cut_rows, flag_rows)


def on_device(adjoint, depth, zonal_coef, merid_coef, coriolis, layer_weight, cutoffs, polar_flags):
    fields, level_count, lat_rows, lon_cells = adjoint.shape
    lat_index = lax.axis_index("lat")
    lat_total = lat_rows * lax.axis_size("lat")
    stacked = adjoint.reshape(fields * level_count, lat_rows, lon_cells)
    bands = lax.all_to_all(stacked, "lat", split_axis=0, concat_axis=1, tiled=True)
    groups = bands.shape[0]
    polar_block = jnp.concatenate([bands[:, :POLE_ROWS], bands[:, lat_total - POLE_ROWS :]], axis=1)
    polar_cuts = jnp.concatenate([cutoffs[:POLE_ROWS], cutoffs[lat_total - POLE_ROWS :]])
    polar_marks = jnp.concatenate([polar_flags[:POLE_ROWS], polar_flags[lat_total - POLE_ROWS :]])
    row_data = polar_block.reshape(groups * 2 * POLE_ROWS, lon_cells)
    cut_rows = jnp.tile(polar_cuts, groups)
    flag_rows = jnp.tile(polar_marks, groups)
    treated = polar_filter(row_data, cut_rows, flag_rows)
    treated = treated.reshape(groups, 2 * POLE_ROWS, lon_cells)
    bands = jnp.concatenate(
        [
            treated[:, :POLE_ROWS],
            bands[:, POLE_ROWS : lat_total - POLE_ROWS],
            treated[:, POLE_ROWS:],
        ],
        axis=1,
    )
    filtered = lax.all_to_all(bands, "lat", split_axis=1, concat_axis=0, tiled=True).reshape(
        adjoint.shape
    )
    q_height = filtered[0]
    q_east = filtered[1]
    q_north = filtered[2]
    zonal_rows = lax.dynamic_slice_in_dim(zonal_coef, lat_index * lat_rows, lat_rows)[None, :, None]
    merid_rows = lax.dynamic_slice_in_dim(merid_coef, lat_index * lat_rows, lat_rows)[None, :, None]
    coriolis_rows = lax.dynamic_slice_in_dim(coriolis, lat_index * lat_rows, lat_rows)[
        None, :, None
    ]
    height_flux = depth.astype(jnp.float32) * q_height
    north_pair = jnp.stack([merid_rows * q_north, merid_rows * height_flux])
    north_rims = extended(north_pair, (("lat", 2),), 1, False)
    merid_diff = north_rims[:, :, :-2] - north_rims[:, :, 2:]
    east_pair = jnp.stack([q_east, height_flux])
    east_rims = extended(east_pair, (("lon", 3),), 1, True)
    zonal_diff = zonal_rows * (east_rims[..., :-2] - east_rims[..., 2:])
    column_force = -zonal_diff[0] - merid_diff[0]
    running = jnp.cumsum(column_force, axis=0)
    carried = entering(
        jnp.sum(column_force, axis=0), "lev", jnp.add, jnp.zeros((lat_rows, lon_cells), jnp.float32)
    )
    new_height = adjoint[0] + layer_weight[:, None, None] * (running + carried[None])
    new_east = adjoint[1] - zonal_diff[1] - coriolis_rows * q_north
    new_north = adjoint[2] - merid_diff[1] + coriolis_rows * q_east
    return jnp.stack([new_height, new_east, new_north])


REMOTE = 28
OWN = 28
OTHER = 30
FAR = 32
TILE = 256
LANES = 128
ROWS = 8
ORDER = (2, 0, 1)
MESH = pl.DeviceIdType.MESH


def halves(value):
    high = value.astype(jnp.bfloat16)
    return high, (value - high.astype(jnp.float32)).astype(jnp.bfloat16)


def split_table(value):
    high = np.asarray(value, np.float32).astype(ml_dtypes.bfloat16)
    low = (np.asarray(value, np.float32) - high.astype(np.float32)).astype(ml_dtypes.bfloat16)
    return high, low


def factors(matrix, rank):
    u, s, v = np.linalg.svd(matrix, full_matrices=False)
    size = np.sqrt(s[:rank])
    return u[:, :rank] * size, v[:rank].T * size


@functools.lru_cache(maxsize=None)
def kernel_tables(cells):
    circle = 2 * cells

    def kernel(distance):
        wave = circle * np.sin(np.pi * (distance % (2 * circle)) / circle)
        return np.where(distance % circle == 0, 0.0, 1.0 / np.where(distance % circle == 0, 1.0, wave))

    n = np.arange(cells)
    here = kernel(n[:, None] - n[None, :])
    project = np.zeros((cells, LANES))
    expand = np.zeros((LANES, cells))
    left, right = factors(kernel(n[:, None] - n[None, :] - cells), REMOTE)
    project[:, :REMOTE] = right
    expand[:REMOTE] = left.T
    project[:, OWN] = kernel(cells - 1 - n)
    project[:, OWN + 1] = kernel(0 - n)
    project[:, OTHER] = kernel(cells - 1 - n - cells)
    project[:, OTHER + 1] = kernel(0 - n - cells)
    blocks = cells // TILE
    at = FAR
    for block in range(blocks):
        part = slice(block * TILE, (block + 1) * TILE)
        far = here[part].copy()
        far[:, part] = 0.0
        rank = 12 if block in (0, blocks - 1) else 18
        left, right = factors(far, rank)
        project[:, at : at + rank] = right
        expand[at : at + rank, part] = left.T
        at += rank
    near = kernel(n[:TILE, None] - n[None, :TILE]).T
    project_high, project_low = split_table(project)
    expand_high, expand_low = split_table(expand)
    near_high, near_low = split_table(near)
    return (
        np.concatenate([project_high, project_low], axis=1),
        np.concatenate([expand_high, expand_high, expand_low]),
        np.concatenate([near_high, near_high, near_low]),
    )


def column(ref, first, kind=jnp.float32):
    row = lax.broadcasted_iota(jnp.int32, (ROWS, LANES), 0)
    value = jnp.zeros((ROWS, LANES), kind)
    for turn in range(ROWS):
        value = jnp.where(row == turn, ref[first + turn], value)
    return value


def across(value, width):
    return jnp.concatenate([value] * (width // LANES), axis=1)


def filter_kernel(
    merid_hbm, cuts_hbm, flags_hbm, x_hbm, depth_hbm, project_hbm, expand_hbm, near_hbm,
    q_ref, rims_ref, edges_ref,
    merid_ref, cuts_ref, flags_ref, x_ref, depth_ref, project_ref, expand_ref, near_ref, high_ref, low_ref, code_ref, edge_ref, send_ref, take_ref,
    rows_ref, brink_ref, scalar_sem, load_sem, table_sem, out_sem, in_sem, up_sem, up_in_sem, down_sem, down_in_sem,
):
    fields, levels, rows, cells = x_ref.shape
    circle = 2 * cells
    count = levels * rows
    half = count // 2
    lat_count = lax.axis_size("lat")
    lat = lax.axis_index("lat")
    lon = lax.axis_index("lon")
    scalars = [
        pltpu.make_async_copy(source, target, scalar_sem.at[turn])
        for turn, (source, target) in enumerate(
            ((cuts_hbm, cuts_ref), (flags_hbm, flags_ref), (merid_hbm, merid_ref))
        )
    ]
    for scalar in scalars:
        scalar.start()
    loads = [pltpu.make_async_copy(x_hbm.at[f], x_ref.at[f], load_sem.at[f]) for f in range(fields)]
    tables = [
        pltpu.make_async_copy(source, target, table_sem.at[turn])
        for turn, (source, target) in enumerate(
            ((project_hbm, project_ref), (depth_hbm, depth_ref), (near_hbm, near_ref), (expand_hbm, expand_ref))
        )
    ]
    loads[ORDER[0]].start()
    tables[0].start()
    loads[ORDER[1]].start()
    tables[1].start()
    loads[ORDER[2]].start()
    tables[2].start()
    tables[3].start()

    barrier = pltpu.get_barrier_semaphore()
    pl.semaphore_signal(barrier, inc=1, device_id={"lon": 1 - lon}, device_id_type=MESH)

    @pl.when(lat > 0)
    def _():
        pl.semaphore_signal(barrier, inc=1, device_id={"lat": lat - 1}, device_id_type=MESH)

    @pl.when(lat < lat_count - 1)
    def _():
        pl.semaphore_signal(barrier, inc=1, device_id={"lat": lat + 1}, device_id_type=MESH)

    for scalar in scalars:
        scalar.wait()
    first = lat * rows
    cuts = column(cuts_ref, first, jnp.int32)
    on = jnp.where(column(flags_ref, first, jnp.int32) > 0, 1.0, 0.0)
    merid = column(merid_ref, first)
    kept = (2 * cuts + 1).astype(jnp.float32)
    keep = jnp.where(on > 0.0, kept * (1.0 / circle), 1.0)
    odd = jnp.bitwise_and(cuts, 1)
    sign = on * jnp.where(odd == 0, -1.0, 1.0)
    place = lax.broadcasted_iota(jnp.int32, (rows, cells), 1).astype(jnp.float32)
    phase = across(kept, cells) * place
    phase = phase - jnp.floor(phase * (1.0 / (2 * circle))) * (2.0 * circle)
    angle = phase * (math.pi / circle)
    cos = across(on, cells) * jnp.cos(angle)
    sin = across(on, cells) * jnp.sin(angle)
    lane = lax.broadcasted_iota(jnp.int32, (rows, LANES), 1)

    def at_edges(end, start, low):
        return jnp.where(lane == low, end, jnp.where(lane == low + 1, start, 0.0))

    end_cos, end_sin = cos[:, cells - 1 :], sin[:, cells - 1 :]
    start_cos, start_sin = cos[:, :1], sin[:, :1]
    mix_cos = at_edges(end_sin, start_sin, OWN) + at_edges(sign * end_cos, sign * start_cos, OTHER)
    mix_sin = at_edges(-end_cos, -start_cos, OWN) + at_edges(sign * end_sin, sign * start_sin, OTHER)
    rows_ref[0] = cos
    rows_ref[1] = sin

    def exchange(field):
        return pltpu.make_async_remote_copy(
            src_ref=send_ref.at[field], dst_ref=take_ref.at[field], send_sem=out_sem.at[field],
            recv_sem=in_sem.at[field], device_id={"lon": 1 - lon}, device_id_type=MESH,
        )

    def spread(value):
        return jnp.broadcast_to(value[None], (levels,) + value.shape).reshape(count, value.shape[1])

    def climb(which):
        return pltpu.make_async_remote_copy(
            src_ref=brink_ref.at[1, which], dst_ref=edges_ref.at[0, which], send_sem=up_sem.at[which],
            recv_sem=up_in_sem.at[which], device_id={"lat": lat + 1}, device_id_type=MESH,
        )

    def descend(which):
        return pltpu.make_async_remote_copy(
            src_ref=brink_ref.at[0, which], dst_ref=edges_ref.at[1, which], send_sem=down_sem.at[which],
            recv_sem=down_in_sem.at[which], device_id={"lat": lat - 1}, device_id_type=MESH,
        )

    lane_all = lax.broadcasted_iota(jnp.int32, (count, LANES), 1)
    part = 8
    for turn, field in enumerate(ORDER):
        loads[field].wait()
        for group in range(levels // part):
            x = x_ref[field, group * part : (group + 1) * part]
            for which in range(2):
                high, low = halves((x * rows_ref[which][None]).reshape(part * rows, cells))
                at = slice(which * count + group * part * rows, which * count + (group + 1) * part * rows)
                high_ref[field, at] = high
                low_ref[field, at] = low
        if turn == 0:
            tables[0].wait()
        table = project_ref[...]
        total = jnp.dot(high_ref[field], table, preferred_element_type=jnp.float32)
        total = total + jnp.dot(low_ref[field], table, preferred_element_type=jnp.float32)
        code = total[:, :LANES] + total[:, LANES:]
        code_ref[field] = code
        code_cos, code_sin = code[:count], code[count:]
        message = jnp.where(lane_all < 32, code_cos, pltpu.roll(code_sin, 32, 1))
        if field < 2:
            edge = spread(mix_cos) * code_cos + spread(mix_sin) * code_sin
            start, end = x_ref[field, :, :, :LANES], x_ref[field, :, :, cells - LANES :]
            start, end = start.reshape(count, LANES)[:, :1], end.reshape(count, LANES)[:, LANES - 1 :]
            edge = edge + spread(keep) * jnp.where(lane_all == OWN, end, jnp.where(lane_all == OWN + 1, start, 0.0))
            edge_ref[field] = edge
            message = jnp.where(jnp.logical_and(lane_all >= OWN, lane_all < OWN + 2), edge, message)
        if field == 0:
            tables[1].wait()
            start, end = depth_ref[:, :, :LANES], depth_ref[:, :, cells - LANES :]
            start = start.astype(jnp.float32).reshape(count, LANES)[:, :1]
            end = end.astype(jnp.float32).reshape(count, LANES)[:, LANES - 1 :]
            message = jnp.where(lane_all == OWN + 32, end, jnp.where(lane_all == OWN + 33, start, message))
        send_ref[field] = jnp.where(lane_all[:half] < 64, message[:half], pltpu.roll(message[half:], 64, 1))
        if turn == 0:
            greeted = 1 + jnp.where(lat > 0, 1, 0) + jnp.where(lat < lat_count - 1, 1, 0)
            pl.semaphore_wait(barrier, greeted)
        exchange(field).start()

    @pl.when(lat == 0)
    def _():
        edges_ref[0] = jnp.zeros(edges_ref.shape[1:], jnp.float32)

    @pl.when(lat == lat_count - 1)
    def _():
        edges_ref[1] = jnp.zeros(edges_ref.shape[1:], jnp.float32)

    tables[2].wait()
    tables[3].wait()
    for field in ORDER:
        exchange(field).wait_recv()
        taken = take_ref[field]
        taken = jnp.concatenate([taken, pltpu.roll(taken, 64, 1)])
        turned = pltpu.roll(taken, 96, 1)
        if field < 2:
            rims = taken + pltpu.roll(edge_ref[field], LANES - 2, 1)
            if field == 0:
                rims = rims * turned
            rims_ref[field] = rims.reshape(levels, rows, LANES)
        signs = spread(sign)
        code = code_ref[field]
        code = jnp.concatenate(
            [
                jnp.where(lane_all < REMOTE, signs * turned, code[:count]),
                jnp.where(lane_all < REMOTE, -signs * taken, code[count:]),
            ]
        )
        code_high, code_low = halves(code)
        for block in range(cells // TILE):
            at = slice(block * TILE, (block + 1) * TILE)
            high, low = high_ref[field, :, at], low_ref[field, :, at]
            terms = jnp.concatenate([high, low, high, code_high, code_low, code_high], axis=1)
            weights = jnp.concatenate([near_ref[...], expand_ref[:, at]], axis=0)
            value = jnp.dot(terms, weights, preferred_element_type=jnp.float32)
            shape = (levels, rows, TILE)
            result = across(keep, TILE)[None] * x_ref[field, :, :, at]
            result = result + rows_ref[1, :, at][None] * value[:count].reshape(shape)
            result = result - rows_ref[0, :, at][None] * value[count:].reshape(shape)
            q_ref[field, :, :, at] = result
            if field != 1:
                edge = result
                if field == 0:
                    edge = result * depth_ref[:, :, at].astype(jnp.float32)
                edge = edge * across(merid, TILE)[None]
                which = 0 if field == 2 else 1
                brink_ref[0, which, :, at] = edge[:, 0, :]
                brink_ref[1, which, :, at] = edge[:, rows - 1, :]
        if field != 1:
            which = 0 if field == 2 else 1

            @pl.when(lat < lat_count - 1)
            def _():
                climb(which).start()

            @pl.when(lat > 0)
            def _():
                descend(which).start()

    for field in ORDER:
        exchange(field).wait_send()

    @pl.when(lat < lat_count - 1)
    def _():
        for which in range(2):
            climb(which).wait_send()
            descend(which).wait_recv()

    @pl.when(lat > 0)
    def _():
        for which in range(2):
            descend(which).wait_send()
            climb(which).wait_recv()


def final_kernel(
    zonal_ref, merid_ref, coriolis_ref, weight_ref, x_ref, q_ref, depth_ref, edges_ref, rims_ref, out_ref, run_ref
):
    step = pl.program_id(0)
    _, levels, rows, cells = out_ref.shape
    first = lax.axis_index("lat") * rows
    zonal = across(column(zonal_ref, first), cells)
    merid = across(column(merid_ref, first), cells)
    coriolis = across(column(coriolis_ref, first), cells)
    row = lax.broadcasted_iota(jnp.int32, (rows, cells), 0)
    lane = lax.broadcasted_iota(jnp.int32, (rows, cells), 1)

    def zonal_adjoint(value, west, east):
        left = jnp.where(lane == 0, west, pltpu.roll(value, 1, 1))
        right = jnp.where(lane == cells - 1, east, pltpu.roll(value, cells - 1, 1))
        return zonal * (left - right)

    def merid_adjoint(value, before, after):
        value = merid * value
        up = jnp.where(row == 0, before, pltpu.roll(value, 1, 0))
        down = jnp.where(row == rows - 1, after, pltpu.roll(value, rows - 1, 0))
        return up - down

    @pl.when(step == 0)
    def _():
        run_ref[...] = jnp.zeros_like(run_ref)

    run = run_ref[...]
    for turn in range(levels):
        level = step * levels + turn
        height, east, north = q_ref[0, level], q_ref[1, level], q_ref[2, level]
        flux = depth_ref[level].astype(jnp.float32) * height
        line = pl.ds(level, 1)
        flux_rims, east_rims = rims_ref[0, level], rims_ref[1, level]
        run = run - (
            zonal_adjoint(east, east_rims[:, OWN : OWN + 1], east_rims[:, OWN + 1 : OWN + 2])
            + merid_adjoint(north, edges_ref[0, 0, line, :], edges_ref[1, 0, line, :])
        )
        out_ref[0, turn] = x_ref[0, level] + weight_ref[level] * run
        out_ref[1, turn] = (
            x_ref[1, level]
            - zonal_adjoint(flux, flux_rims[:, OWN : OWN + 1], flux_rims[:, OWN + 1 : OWN + 2])
            - coriolis * north
        )
        out_ref[2, turn] = (
            x_ref[2, level]
            - merid_adjoint(flux, edges_ref[0, 1, line, :], edges_ref[1, 1, line, :])
            + coriolis * east
        )
    run_ref[...] = run


def on_pair(adjoint, depth, zonal_coef, merid_coef, coriolis, layer_weight, cutoffs, polar_flags):
    fields, level_count, rows, cells = adjoint.shape
    project, expand, near = (jnp.asarray(table) for table in kernel_tables(cells))
    count = level_count * rows
    scalars = pl.BlockSpec(memory_space=pltpu.SMEM)
    there = pl.BlockSpec(memory_space=pltpu.HBM)
    close = pl.BlockSpec(memory_space=pltpu.VMEM)
    single = jnp.float32
    dma = pltpu.SemaphoreType.DMA

    q, rims, edges = pl.pallas_call(
        filter_kernel,
        in_specs=[there] * 8,
        out_specs=[close] * 3,
        out_shape=[
            jax.ShapeDtypeStruct(adjoint.shape, single),
            jax.ShapeDtypeStruct((2, level_count, rows, LANES), single),
            jax.ShapeDtypeStruct((2, 2, level_count, cells), single),
        ],
        scratch_shapes=[
            pltpu.SMEM(merid_coef.shape, single),
            pltpu.SMEM(cutoffs.shape, jnp.int32),
            pltpu.SMEM(polar_flags.shape, jnp.int32),
            pltpu.VMEM(adjoint.shape, single),
            pltpu.VMEM(depth.shape, depth.dtype),
            pltpu.VMEM(project.shape, project.dtype),
            pltpu.VMEM(expand.shape, expand.dtype),
            pltpu.VMEM(near.shape, near.dtype),
            pltpu.VMEM((fields, 2 * count, cells), jnp.bfloat16),
            pltpu.VMEM((fields, 2 * count, cells), jnp.bfloat16),
            pltpu.VMEM((fields, 2 * count, LANES), single),
            pltpu.VMEM((2, count, LANES), single),
            pltpu.VMEM((fields, count // 2, LANES), single),
            pltpu.VMEM((fields, count // 2, LANES), single),
            pltpu.VMEM((2, rows, cells), single),
            pltpu.VMEM((2, 2, level_count, cells), single),
            dma((3,)),
            dma((3,)),
            dma((4,)),
            dma((3,)),
            dma((3,)),
            dma((2,)),
            dma((2,)),
            dma((2,)),
            dma((2,)),
        ],
        compiler_params=pltpu.CompilerParams(
            collective_id=0, has_side_effects=True, vmem_limit_bytes=36 * 2**20
        ),
    )(*(pltpu.with_memory_space_constraint(value, pltpu.HBM) for value in (merid_coef, cutoffs, polar_flags, adjoint, depth, project, expand, near)))

    part = 8
    four = pl.BlockSpec((fields, part, rows, cells), lambda i: (0, i, 0, 0))
    return pl.pallas_call(
        final_kernel,
        grid=(level_count // part,),
        in_specs=[scalars] * 4 + [close] * 5,
        out_specs=four,
        out_shape=jax.ShapeDtypeStruct(adjoint.shape, single),
        scratch_shapes=[pltpu.VMEM((rows, cells), single)],
        compiler_params=pltpu.CompilerParams(vmem_limit_bytes=32 * 2**20),
    )(zonal_coef, merid_coef, coriolis, layer_weight, adjoint, q, depth, edges, rims)


def plan_for(mesh):
    return on_pair if mesh.shape["lon"] == 2 and mesh.shape["lev"] == 1 else on_device


def solution(mesh):
    return jax.shard_map(
        plan_for(mesh),
        mesh=mesh,
        in_specs=(
            P("member", "lev", "lat", "lon"),
            P("lev", "lat", "lon"),
            P(),
            P(),
            P(),
            P("lev"),
            P(),
            P(),
        ),
        out_specs=P("member", "lev", "lat", "lon"),
        check_vma=False,
    )
```

```python
import functools
import math

import jax
import jax.numpy as jnp
import ml_dtypes
import numpy as np
from jax import lax
from jax.experimental import pallas as pl
from jax.experimental.pallas import tpu as pltpu
from jax.sharding import PartitionSpec as P

KMAX = 1024
POLE_ROWS = 24


def extended(cells, sides, width, closed):
    for axis, dim in sides:
        count = lax.axis_size(axis)
        ends = count if closed else count - 1
        head = lax.slice_in_dim(cells, 0, width, axis=dim)
        tail = lax.slice_in_dim(cells, cells.shape[dim] - width, cells.shape[dim], axis=dim)
        cells = jnp.concatenate(
            [
                lax.ppermute(tail, axis, [(i, (i + 1) % count) for i in range(ends)]),
                cells,
                lax.ppermute(head, axis, [((i + 1) % count, i) for i in range(ends)]),
            ],
            axis=dim,
        )
    return cells


def entering(value, axis, join, neutral):
    count, mine = (lax.axis_size(axis), lax.axis_index(axis))
    pieces = lax.all_gather(value, axis)
    total = jnp.full_like(value, 0) + jnp.asarray(neutral, value.dtype)

    def turn(position, total):
        longer = join(total, pieces[position])
        return jnp.where(position < mine, longer, total)

    return lax.fori_loop(0, count - 1, turn, total)


def wave_table(col_count, wave_start, wave_count, circle):
    columns = lax.iota(jnp.int32, col_count)
    wave_index = wave_start + lax.iota(jnp.int32, wave_count)
    phase = columns[:, None] * wave_index[None, :] % circle
    angle = phase.astype(jnp.float32) * (2.0 * math.pi / circle)
    return jnp.concatenate([jnp.cos(angle), jnp.sin(angle)], axis=1)


def keep_weights(cut_rows, wave_start, wave_count, circle):
    wave_index = wave_start + lax.iota(jnp.int32, wave_count)
    factor = jnp.where(wave_index == 0, 1.0, 2.0) / circle
    kept = (wave_index[None, :] <= cut_rows[:, None]).astype(jnp.float32) * factor[None, :]
    return jnp.concatenate([kept, kept], axis=1)


def block_width():
    return min(KMAX, 128)


def project_rows(row_data, cut_rows):
    circle = row_data.shape[1]
    width = block_width()
    result = jnp.zeros(row_data.shape, jnp.float32)
    for block_index in range(KMAX // width):
        table = wave_table(circle, block_index * width, width, circle)
        coefs = jnp.dot(
            row_data, table, precision=lax.Precision.HIGHEST, preferred_element_type=jnp.float32
        )
        weights = keep_weights(cut_rows, block_index * width, width, circle)
        result = result + jnp.dot(
            coefs * weights,
            table.T,
            precision=lax.Precision.HIGHEST,
            preferred_element_type=jnp.float32,
        )
    return result


def transpose_filter(row_data, cut_rows, flag_rows):
    lon_count = lax.axis_size("lon")
    lon_index = lax.axis_index("lon")
    share = row_data.shape[0] // lon_count
    full_rows = lax.all_to_all(row_data, "lon", split_axis=0, concat_axis=1, tiled=True)
    my_cuts = lax.dynamic_slice_in_dim(cut_rows, lon_index * share, share)
    smoothed = project_rows(full_rows, my_cuts)
    returned = lax.all_to_all(smoothed, "lon", split_axis=1, concat_axis=0, tiled=True)
    return jnp.where(flag_rows[:, None] > 0, returned, row_data)


def polar_filter(row_data, cut_rows, flag_rows):
    return transpose_filter(row_data, cut_rows, flag_rows)


def on_device(adjoint, depth, zonal_coef, merid_coef, coriolis, layer_weight, cutoffs, polar_flags):
    fields, level_count, lat_rows, lon_cells = adjoint.shape
    lat_index = lax.axis_index("lat")
    lat_total = lat_rows * lax.axis_size("lat")
    stacked = adjoint.reshape(fields * level_count, lat_rows, lon_cells)
    bands = lax.all_to_all(stacked, "lat", split_axis=0, concat_axis=1, tiled=True)
    groups = bands.shape[0]
    polar_block = jnp.concatenate([bands[:, :POLE_ROWS], bands[:, lat_total - POLE_ROWS :]], axis=1)
    polar_cuts = jnp.concatenate([cutoffs[:POLE_ROWS], cutoffs[lat_total - POLE_ROWS :]])
    polar_marks = jnp.concatenate([polar_flags[:POLE_ROWS], polar_flags[lat_total - POLE_ROWS :]])
    row_data = polar_block.reshape(groups * 2 * POLE_ROWS, lon_cells)
    cut_rows = jnp.tile(polar_cuts, groups)
    flag_rows = jnp.tile(polar_marks, groups)
    treated = polar_filter(row_data, cut_rows, flag_rows)
    treated = treated.reshape(groups, 2 * POLE_ROWS, lon_cells)
    bands = jnp.concatenate(
        [
            treated[:, :POLE_ROWS],
            bands[:, POLE_ROWS : lat_total - POLE_ROWS],
            treated[:, POLE_ROWS:],
        ],
        axis=1,
    )
    filtered = lax.all_to_all(bands, "lat", split_axis=1, concat_axis=0, tiled=True).reshape(
        adjoint.shape
    )
    q_height = filtered[0]
    q_east = filtered[1]
    q_north = filtered[2]
    zonal_rows = lax.dynamic_slice_in_dim(zonal_coef, lat_index * lat_rows, lat_rows)[None, :, None]
    merid_rows = lax.dynamic_slice_in_dim(merid_coef, lat_index * lat_rows, lat_rows)[None, :, None]
    coriolis_rows = lax.dynamic_slice_in_dim(coriolis, lat_index * lat_rows, lat_rows)[
        None, :, None
    ]
    height_flux = depth.astype(jnp.float32) * q_height
    north_pair = jnp.stack([merid_rows * q_north, merid_rows * height_flux])
    north_rims = extended(north_pair, (("lat", 2),), 1, False)
    merid_diff = north_rims[:, :, :-2] - north_rims[:, :, 2:]
    east_pair = jnp.stack([q_east, height_flux])
    east_rims = extended(east_pair, (("lon", 3),), 1, True)
    zonal_diff = zonal_rows * (east_rims[..., :-2] - east_rims[..., 2:])
    column_force = -zonal_diff[0] - merid_diff[0]
    running = jnp.cumsum(column_force, axis=0)
    carried = entering(
        jnp.sum(column_force, axis=0), "lev", jnp.add, jnp.zeros((lat_rows, lon_cells), jnp.float32)
    )
    new_height = adjoint[0] + layer_weight[:, None, None] * (running + carried[None])
    new_east = adjoint[1] - zonal_diff[1] - coriolis_rows * q_north
    new_north = adjoint[2] - merid_diff[1] + coriolis_rows * q_east
    return jnp.stack([new_height, new_east, new_north])


REMOTE = 28
OWN = 28
OTHER = 30
FAR = 32
CODES = 80
GROUP = 2
TILE = 256
LANES = 128
ROWS = 8
ORDER = (2, 0, 1)
MESH = pl.DeviceIdType.MESH


def halves(value):
    high = value.astype(jnp.bfloat16)
    return high, (value - high.astype(jnp.float32)).astype(jnp.bfloat16)


def split_table(value):
    high = np.asarray(value, np.float32).astype(ml_dtypes.bfloat16)
    low = (np.asarray(value, np.float32) - high.astype(np.float32)).astype(ml_dtypes.bfloat16)
    return high, low


def factors(matrix, rank):
    u, s, v = np.linalg.svd(matrix, full_matrices=False)
    size = np.sqrt(s[:rank])
    return u[:, :rank] * size, v[:rank].T * size


@functools.lru_cache(maxsize=None)
def kernel_tables(cells):
    circle = 2 * cells

    def kernel(distance):
        wave = circle * np.sin(np.pi * (distance % (2 * circle)) / circle)
        return np.where(distance % circle == 0, 0.0, 1.0 / np.where(distance % circle == 0, 1.0, wave))

    n = np.arange(cells)
    here = kernel(n[:, None] - n[None, :])
    project = np.zeros((cells, LANES))
    expand = np.zeros((LANES, cells))
    left, right = factors(kernel(n[:, None] - n[None, :] - cells), REMOTE)
    project[:, :REMOTE] = right
    expand[:REMOTE] = left.T
    project[:, OWN] = kernel(cells - 1 - n)
    project[:, OWN + 1] = kernel(0 - n)
    project[:, OTHER] = kernel(cells - 1 - n - cells)
    project[:, OTHER + 1] = kernel(0 - n - cells)
    blocks = cells // TILE
    at = FAR
    for block in range(blocks):
        part = slice(block * TILE, (block + 1) * TILE)
        far = here[part].copy()
        far[:, part] = 0.0
        rank = 12 if block in (0, blocks - 1) else 18
        left, right = factors(far, rank)
        project[:, at : at + rank] = right
        expand[at : at + rank, part] = left.T
        at += rank
    split = cells // 2
    turned = np.roll(expand, 48, axis=0)
    groups = []
    for part in (expand[:CODES, :split], turned[:CODES, split:]):
        high, low = split_table(part)
        groups.append(np.concatenate([high, high, low, np.zeros((TILE - 3 * CODES, split), high.dtype)]))
    near = kernel(n[:TILE, None] - n[None, :TILE]).T
    project_high, project_low = split_table(project)
    near_high, near_low = split_table(near)
    return (
        np.concatenate([project_high, project_low], axis=1),
        np.concatenate(groups, axis=1),
        np.concatenate([near_high, near_high, near_low]),
    )


def column(ref, first, kind=jnp.float32):
    row = lax.broadcasted_iota(jnp.int32, (ROWS, LANES), 0)
    value = jnp.zeros((ROWS, LANES), kind)
    for turn in range(ROWS):
        value = jnp.where(row == turn, ref[first + turn], value)
    return value


def across(value, width):
    return jnp.concatenate([value] * (width // LANES), axis=1)


def filter_kernel(
    merid_hbm, cuts_hbm, flags_hbm, x_hbm, depth_hbm, project_hbm, expand_hbm, near_hbm,
    q_ref, rims_ref, edges_ref, x_ref, depth_ref,
    merid_ref, cuts_ref, flags_ref, project_ref, expand_ref, near_ref, high_ref, low_ref, code_ref, edge_ref, send_ref, take_ref,
    rows_ref, brink_ref, scalar_sem, load_sem, table_sem, out_sem, in_sem, leave_sem, reach_sem,
):
    fields, levels, rows, cells = x_ref.shape
    circle = 2 * cells
    count = levels * rows
    half = count // 2
    lat_count = lax.axis_size("lat")
    lat = lax.axis_index("lat")
    lon = lax.axis_index("lon")
    scalars = [
        pltpu.make_async_copy(source, target, scalar_sem.at[turn])
        for turn, (source, target) in enumerate(
            ((cuts_hbm, cuts_ref), (flags_hbm, flags_ref), (merid_hbm, merid_ref))
        )
    ]
    for scalar in scalars:
        scalar.start()
    loads = [pltpu.make_async_copy(x_hbm.at[f], x_ref.at[f], load_sem.at[f]) for f in range(fields)]
    tables = [
        pltpu.make_async_copy(source, target, table_sem.at[turn])
        for turn, (source, target) in enumerate(
            ((project_hbm, project_ref), (depth_hbm, depth_ref), (near_hbm, near_ref), (expand_hbm, expand_ref))
        )
    ]
    loads[ORDER[0]].start()
    tables[0].start()
    loads[ORDER[1]].start()
    tables[1].start()
    loads[ORDER[2]].start()
    tables[2].start()
    tables[3].start()

    barrier = pltpu.get_barrier_semaphore()
    pl.semaphore_signal(barrier, inc=1, device_id={"lon": 1 - lon}, device_id_type=MESH)

    up = {"lat": jnp.minimum(lat + 1, lat_count - 1), "lon": jnp.where(lat < lat_count - 1, lon, 1 - lon)}
    down = {"lat": jnp.maximum(lat - 1, 0), "lon": jnp.where(lat > 0, lon, 1 - lon)}
    upward = [lat % 2, 1 - lat % 2]
    targets = [{name: jnp.where(way == 1, up[name], down[name]) for name in up} for way in upward]
    slots = [
        jnp.where(way == 1, jnp.where(lat < lat_count - 1, 0, 1), jnp.where(lat > 0, 1, 0)) for way in upward
    ]
    for target in targets:
        pl.semaphore_signal(barrier, inc=1, device_id=target, device_id_type=MESH)

    for scalar in scalars:
        scalar.wait()
    first = lat * rows
    cuts = column(cuts_ref, first, jnp.int32)
    on = jnp.where(column(flags_ref, first, jnp.int32) > 0, 1.0, 0.0)
    at_end = jnp.where(lat == 0, 0, jnp.where(lat == lat_count - 1, rows - 1, -1))
    row = lax.broadcasted_iota(jnp.int32, (rows, LANES), 0)
    brink = jnp.where(row == at_end, 0.0, column(merid_ref, first))
    kept = (2 * cuts + 1).astype(jnp.float32)
    keep = jnp.where(on > 0.0, kept * (1.0 / circle), 1.0)
    odd = jnp.bitwise_and(cuts, 1)
    sign = on * jnp.where(odd == 0, -1.0, 1.0)
    place = lax.broadcasted_iota(jnp.int32, (rows, cells), 1).astype(jnp.float32)
    phase = across(kept, cells) * place
    phase = phase - jnp.floor(phase * (1.0 / (2 * circle))) * (2.0 * circle)
    angle = phase * (math.pi / circle)
    cos = across(on, cells) * jnp.cos(angle)
    sin = across(on, cells) * jnp.sin(angle)
    lane = lax.broadcasted_iota(jnp.int32, (rows, LANES), 1)

    def at_edges(end, start, low):
        return jnp.where(lane == low, end, jnp.where(lane == low + 1, start, 0.0))

    end_cos, end_sin = cos[:, cells - 1 :], sin[:, cells - 1 :]
    start_cos, start_sin = cos[:, :1], sin[:, :1]
    mix_cos = at_edges(end_sin, start_sin, OWN) + at_edges(sign * end_cos, sign * start_cos, OTHER)
    mix_sin = at_edges(-end_cos, -start_cos, OWN) + at_edges(sign * end_sin, sign * start_sin, OTHER)
    rows_ref[0] = cos
    rows_ref[1] = sin

    def exchange(field):
        return pltpu.make_async_remote_copy(
            src_ref=send_ref.at[field], dst_ref=take_ref.at[field], send_sem=out_sem.at[field],
            recv_sem=in_sem.at[field], device_id={"lon": 1 - lon}, device_id_type=MESH,
        )

    def spread(value):
        return jnp.broadcast_to(value[None], (levels,) + value.shape).reshape(count, value.shape[1])

    groups = cells // TILE // GROUP

    def send(turn, which, group, slot):
        at = pl.ds(group * GROUP * TILE, GROUP * TILE)
        place = which * groups + group
        return pltpu.make_async_remote_copy(
            src_ref=brink_ref.at[upward[turn], which, :, at], dst_ref=edges_ref.at[slot, which, :, at],
            send_sem=leave_sem.at[turn, place], recv_sem=reach_sem.at[slot, place],
            device_id=targets[turn], device_id_type=MESH,
        )

    lane_all = lax.broadcasted_iota(jnp.int32, (count, LANES), 1)
    part = 8
    for turn, field in enumerate(ORDER):
        loads[field].wait()
        for group in range(levels // part):
            x = x_ref[field, group * part : (group + 1) * part]
            for which in range(2):
                high, low = halves((x * rows_ref[which][None]).reshape(part * rows, cells))
                at = slice(which * count + group * part * rows, which * count + (group + 1) * part * rows)
                high_ref[field, at] = high
                low_ref[field, at] = low
        if turn == 0:
            tables[0].wait()
        table = project_ref[...]
        total = jnp.dot(high_ref[field], table, preferred_element_type=jnp.float32)
        total = total + jnp.dot(low_ref[field], table, preferred_element_type=jnp.float32)
        code = total[:, :LANES] + total[:, LANES:]
        code_ref[field] = code
        code_cos, code_sin = code[:count], code[count:]
        message = jnp.where(lane_all < 32, code_cos, pltpu.roll(code_sin, 32, 1))
        if field < 2:
            edge = spread(mix_cos) * code_cos + spread(mix_sin) * code_sin
            start, end = x_ref[field, :, :, :LANES], x_ref[field, :, :, cells - LANES :]
            start, end = start.reshape(count, LANES)[:, :1], end.reshape(count, LANES)[:, LANES - 1 :]
            edge = edge + spread(keep) * jnp.where(lane_all == OWN, end, jnp.where(lane_all == OWN + 1, start, 0.0))
            edge_ref[field] = edge
            message = jnp.where(jnp.logical_and(lane_all >= OWN, lane_all < OWN + 2), edge, message)
        if field == 0:
            tables[1].wait()
            start, end = depth_ref[:, :, :LANES], depth_ref[:, :, cells - LANES :]
            start = start.astype(jnp.float32).reshape(count, LANES)[:, :1]
            end = end.astype(jnp.float32).reshape(count, LANES)[:, LANES - 1 :]
            message = jnp.where(lane_all == OWN + 32, end, jnp.where(lane_all == OWN + 33, start, message))
        send_ref[field] = jnp.where(lane_all[:half] < 64, message[:half], pltpu.roll(message[half:], 64, 1))
        if turn == 0:
            pl.semaphore_wait(barrier, 3)
        exchange(field).start()

    tables[2].wait()
    tables[3].wait()
    for field in ORDER:
        exchange(field).wait_recv()
        taken = take_ref[field]
        taken = jnp.concatenate([taken, pltpu.roll(taken, 64, 1)])
        turned = pltpu.roll(taken, 96, 1)
        if field < 2:
            rims = taken + pltpu.roll(edge_ref[field], LANES - 2, 1)
            if field == 0:
                rims = rims * turned
            rims = jnp.where(
                lane_all == LANES - 1, pltpu.roll(rims, LANES - 2 - OWN, 1), pltpu.roll(rims, LANES - OWN, 1)
            )
            rims_ref[field] = rims.reshape(levels, rows, LANES)
        signs = spread(sign)
        code = code_ref[field]
        code = jnp.concatenate(
            [
                jnp.where(lane_all < REMOTE, signs * turned, code[:count]),
                jnp.where(lane_all < REMOTE, -signs * taken, code[count:]),
            ]
        )
        code_high = code.astype(jnp.bfloat16).astype(jnp.float32)
        code_low = code - code_high
        lane_both = lax.broadcasted_iota(jnp.int32, code.shape, 1)
        packed = []
        for low, head, rest in (
            (pltpu.roll(code_low, CODES, 1), code_high, pltpu.roll(code_high, 32, 1)),
            (code_low, pltpu.roll(code_high, 48, 1), pltpu.roll(code_high, 80, 1)),
        ):
            pair = (jnp.where(lane_both < CODES, head, low), jnp.where(lane_both < 32, low, rest))
            packed.append([value.astype(jnp.bfloat16) for value in pair])
        for block in range(cells // TILE):
            at = slice(block * TILE, (block + 1) * TILE)
            high, low = high_ref[field, :, at], low_ref[field, :, at]
            terms = jnp.concatenate([high, low, high, *packed[2 * at.start // cells]], axis=1)
            weights = jnp.concatenate([near_ref[...], expand_ref[:, at]], axis=0)
            value = jnp.dot(terms, weights, preferred_element_type=jnp.float32)
            shape = (levels, rows, TILE)
            result = across(keep, TILE)[None] * x_ref[field, :, :, at]
            result = result + rows_ref[1, :, at][None] * value[:count].reshape(shape)
            result = result - rows_ref[0, :, at][None] * value[count:].reshape(shape)
            q_ref[field, :, :, at] = result
            if field != 1:
                edge = result
                if field == 0:
                    edge = result * depth_ref[:, :, at].astype(jnp.float32)
                edge = edge * across(brink, TILE)[None]
                which = 0 if field == 2 else 1
                brink_ref[0, which, :, at] = edge[:, 0, :]
                brink_ref[1, which, :, at] = edge[:, rows - 1, :]
                if block % GROUP == GROUP - 1:
                    for turn in range(2):
                        send(turn, which, block // GROUP, slots[turn]).start()

    for field in ORDER:
        exchange(field).wait_send()

    for which in range(2):
        for group in range(groups):
            for turn in range(2):
                send(turn, which, group, slots[turn]).wait_send()
                send(turn, which, group, turn).wait_recv()


def final_kernel(
    zonal_ref, merid_ref, coriolis_ref, weight_ref, x_ref, q_ref, depth_ref, edges_ref, rims_ref, out_ref, run_ref
):
    step = pl.program_id(0)
    _, levels, rows, cells = out_ref.shape
    first = lax.axis_index("lat") * rows
    zonal = across(column(zonal_ref, first), cells)
    merid = across(column(merid_ref, first), cells)
    coriolis = across(column(coriolis_ref, first), cells)
    row = lax.broadcasted_iota(jnp.int32, (rows, cells), 0)
    lane = lax.broadcasted_iota(jnp.int32, (rows, LANES), 1)

    def zonal_adjoint(value, rims):
        left, right = pltpu.roll(value, 1, 1), pltpu.roll(value, cells - 1, 1)
        left = jnp.concatenate([jnp.where(lane == 0, rims, left[:, :LANES]), left[:, LANES:]], axis=1)
        split = cells - LANES
        right = jnp.concatenate([right[:, :split], jnp.where(lane == LANES - 1, rims, right[:, split:])], axis=1)
        return zonal * (left - right)

    def merid_adjoint(value, before, after):
        value = merid * value
        up = jnp.where(row == 0, before, pltpu.roll(value, 1, 0))
        down = jnp.where(row == rows - 1, after, pltpu.roll(value, rows - 1, 0))
        return up - down

    @pl.when(step == 0)
    def _():
        run_ref[...] = jnp.zeros_like(run_ref)

    run = run_ref[...]
    for turn in range(levels):
        level = step * levels + turn
        height, east, north = q_ref[0, level], q_ref[1, level], q_ref[2, level]
        flux = depth_ref[level].astype(jnp.float32) * height
        line = pl.ds(level, 1)
        flux_rims, east_rims = rims_ref[0, level], rims_ref[1, level]
        run = run - (
            zonal_adjoint(east, east_rims)
            + merid_adjoint(north, edges_ref[0, 0, line, :], edges_ref[1, 0, line, :])
        )
        out_ref[0, turn] = x_ref[0, level] + weight_ref[level] * run
        out_ref[1, turn] = (
            x_ref[1, level]
            - zonal_adjoint(flux, flux_rims)
            - coriolis * north
        )
        out_ref[2, turn] = (
            x_ref[2, level]
            - merid_adjoint(flux, edges_ref[0, 1, line, :], edges_ref[1, 1, line, :])
            + coriolis * east
        )
    run_ref[...] = run


def on_pair(adjoint, depth, zonal_coef, merid_coef, coriolis, layer_weight, cutoffs, polar_flags):
    fields, level_count, rows, cells = adjoint.shape
    project, expand, near = (jnp.asarray(table) for table in kernel_tables(cells))
    count = level_count * rows
    pieces = cells // TILE // GROUP
    scalars = pl.BlockSpec(memory_space=pltpu.SMEM)
    there = pl.BlockSpec(memory_space=pltpu.HBM)
    close = pl.BlockSpec(memory_space=pltpu.VMEM)
    single = jnp.float32
    dma = pltpu.SemaphoreType.DMA

    q, rims, edges, adjoint_near, depth_near = pl.pallas_call(
        filter_kernel,
        in_specs=[there] * 8,
        out_specs=[close] * 5,
        out_shape=[
            jax.ShapeDtypeStruct(adjoint.shape, single),
            jax.ShapeDtypeStruct((2, level_count, rows, LANES), single),
            jax.ShapeDtypeStruct((2, 2, level_count, cells), single),
            jax.ShapeDtypeStruct(adjoint.shape, single),
            jax.ShapeDtypeStruct(depth.shape, depth.dtype),
        ],
        scratch_shapes=[
            pltpu.SMEM(merid_coef.shape, single),
            pltpu.SMEM(cutoffs.shape, jnp.int32),
            pltpu.SMEM(polar_flags.shape, jnp.int32),
            pltpu.VMEM(project.shape, project.dtype),
            pltpu.VMEM(expand.shape, expand.dtype),
            pltpu.VMEM(near.shape, near.dtype),
            pltpu.VMEM((fields, 2 * count, cells), jnp.bfloat16),
            pltpu.VMEM((fields, 2 * count, cells), jnp.bfloat16),
            pltpu.VMEM((fields, 2 * count, LANES), single),
            pltpu.VMEM((2, count, LANES), single),
            pltpu.VMEM((fields, count // 2, LANES), single),
            pltpu.VMEM((fields, count // 2, LANES), single),
            pltpu.VMEM((2, rows, cells), single),
            pltpu.VMEM((2, 2, level_count, cells), single),
            dma((3,)),
            dma((3,)),
            dma((4,)),
            dma((3,)),
            dma((3,)),
            dma((2, 2 * pieces)),
            dma((2, 2 * pieces)),
        ],
        compiler_params=pltpu.CompilerParams(
            collective_id=0, has_side_effects=True, vmem_limit_bytes=36 * 2**20
        ),
    )(*(pltpu.with_memory_space_constraint(value, pltpu.HBM) for value in (merid_coef, cutoffs, polar_flags, adjoint, depth, project, expand, near)))

    part = 8
    four = pl.BlockSpec((fields, part, rows, cells), lambda i: (0, i, 0, 0))
    return pl.pallas_call(
        final_kernel,
        grid=(level_count // part,),
        in_specs=[scalars] * 4 + [close] * 5,
        out_specs=four,
        out_shape=jax.ShapeDtypeStruct(adjoint.shape, single),
        scratch_shapes=[pltpu.VMEM((rows, cells), single)],
        compiler_params=pltpu.CompilerParams(vmem_limit_bytes=32 * 2**20),
    )(zonal_coef, merid_coef, coriolis, layer_weight, adjoint_near, q, depth_near, edges, rims)


def plan_for(mesh):
    return on_pair if mesh.shape["lon"] == 2 and mesh.shape["lev"] == 1 else on_device


def solution(mesh):
    return jax.shard_map(
        plan_for(mesh),
        mesh=mesh,
        in_specs=(
            P("member", "lev", "lat", "lon"),
            P("lev", "lat", "lon"),
            P(),
            P(),
            P(),
            P("lev"),
            P(),
            P(),
        ),
        out_specs=P("member", "lev", "lat", "lon"),
        check_vma=False,
    )
```

```python
import functools
import math

import jax
import jax.numpy as jnp
import ml_dtypes
import numpy as np
from jax import lax
from jax.experimental import pallas as pl
from jax.experimental.pallas import tpu as pltpu
from jax.sharding import PartitionSpec as P

KMAX = 1024
POLE_ROWS = 24


def extended(cells, sides, width, closed):
    for axis, dim in sides:
        count = lax.axis_size(axis)
        ends = count if closed else count - 1
        head = lax.slice_in_dim(cells, 0, width, axis=dim)
        tail = lax.slice_in_dim(cells, cells.shape[dim] - width, cells.shape[dim], axis=dim)
        cells = jnp.concatenate(
            [
                lax.ppermute(tail, axis, [(i, (i + 1) % count) for i in range(ends)]),
                cells,
                lax.ppermute(head, axis, [((i + 1) % count, i) for i in range(ends)]),
            ],
            axis=dim,
        )
    return cells


def entering(value, axis, join, neutral):
    count, mine = (lax.axis_size(axis), lax.axis_index(axis))
    pieces = lax.all_gather(value, axis)
    total = jnp.full_like(value, 0) + jnp.asarray(neutral, value.dtype)

    def turn(position, total):
        longer = join(total, pieces[position])
        return jnp.where(position < mine, longer, total)

    return lax.fori_loop(0, count - 1, turn, total)


def wave_table(col_count, wave_start, wave_count, circle):
    columns = lax.iota(jnp.int32, col_count)
    wave_index = wave_start + lax.iota(jnp.int32, wave_count)
    phase = columns[:, None] * wave_index[None, :] % circle
    angle = phase.astype(jnp.float32) * (2.0 * math.pi / circle)
    return jnp.concatenate([jnp.cos(angle), jnp.sin(angle)], axis=1)


def keep_weights(cut_rows, wave_start, wave_count, circle):
    wave_index = wave_start + lax.iota(jnp.int32, wave_count)
    factor = jnp.where(wave_index == 0, 1.0, 2.0) / circle
    kept = (wave_index[None, :] <= cut_rows[:, None]).astype(jnp.float32) * factor[None, :]
    return jnp.concatenate([kept, kept], axis=1)


def block_width():
    return min(KMAX, 128)


def project_rows(row_data, cut_rows):
    circle = row_data.shape[1]
    width = block_width()
    result = jnp.zeros(row_data.shape, jnp.float32)
    for block_index in range(KMAX // width):
        table = wave_table(circle, block_index * width, width, circle)
        coefs = jnp.dot(
            row_data, table, precision=lax.Precision.HIGHEST, preferred_element_type=jnp.float32
        )
        weights = keep_weights(cut_rows, block_index * width, width, circle)
        result = result + jnp.dot(
            coefs * weights,
            table.T,
            precision=lax.Precision.HIGHEST,
            preferred_element_type=jnp.float32,
        )
    return result


def transpose_filter(row_data, cut_rows, flag_rows):
    lon_count = lax.axis_size("lon")
    lon_index = lax.axis_index("lon")
    share = row_data.shape[0] // lon_count
    full_rows = lax.all_to_all(row_data, "lon", split_axis=0, concat_axis=1, tiled=True)
    my_cuts = lax.dynamic_slice_in_dim(cut_rows, lon_index * share, share)
    smoothed = project_rows(full_rows, my_cuts)
    returned = lax.all_to_all(smoothed, "lon", split_axis=1, concat_axis=0, tiled=True)
    return jnp.where(flag_rows[:, None] > 0, returned, row_data)


def polar_filter(row_data, cut_rows, flag_rows):
    return transpose_filter(row_data, cut_rows, flag_rows)


def on_device(adjoint, depth, zonal_coef, merid_coef, coriolis, layer_weight, cutoffs, polar_flags):
    fields, level_count, lat_rows, lon_cells = adjoint.shape
    lat_index = lax.axis_index("lat")
    lat_total = lat_rows * lax.axis_size("lat")
    stacked = adjoint.reshape(fields * level_count, lat_rows, lon_cells)
    bands = lax.all_to_all(stacked, "lat", split_axis=0, concat_axis=1, tiled=True)
    groups = bands.shape[0]
    polar_block = jnp.concatenate([bands[:, :POLE_ROWS], bands[:, lat_total - POLE_ROWS :]], axis=1)
    polar_cuts = jnp.concatenate([cutoffs[:POLE_ROWS], cutoffs[lat_total - POLE_ROWS :]])
    polar_marks = jnp.concatenate([polar_flags[:POLE_ROWS], polar_flags[lat_total - POLE_ROWS :]])
    row_data = polar_block.reshape(groups * 2 * POLE_ROWS, lon_cells)
    cut_rows = jnp.tile(polar_cuts, groups)
    flag_rows = jnp.tile(polar_marks, groups)
    treated = polar_filter(row_data, cut_rows, flag_rows)
    treated = treated.reshape(groups, 2 * POLE_ROWS, lon_cells)
    bands = jnp.concatenate(
        [
            treated[:, :POLE_ROWS],
            bands[:, POLE_ROWS : lat_total - POLE_ROWS],
            treated[:, POLE_ROWS:],
        ],
        axis=1,
    )
    filtered = lax.all_to_all(bands, "lat", split_axis=1, concat_axis=0, tiled=True).reshape(
        adjoint.shape
    )
    q_height = filtered[0]
    q_east = filtered[1]
    q_north = filtered[2]
    zonal_rows = lax.dynamic_slice_in_dim(zonal_coef, lat_index * lat_rows, lat_rows)[None, :, None]
    merid_rows = lax.dynamic_slice_in_dim(merid_coef, lat_index * lat_rows, lat_rows)[None, :, None]
    coriolis_rows = lax.dynamic_slice_in_dim(coriolis, lat_index * lat_rows, lat_rows)[
        None, :, None
    ]
    height_flux = depth.astype(jnp.float32) * q_height
    north_pair = jnp.stack([merid_rows * q_north, merid_rows * height_flux])
    north_rims = extended(north_pair, (("lat", 2),), 1, False)
    merid_diff = north_rims[:, :, :-2] - north_rims[:, :, 2:]
    east_pair = jnp.stack([q_east, height_flux])
    east_rims = extended(east_pair, (("lon", 3),), 1, True)
    zonal_diff = zonal_rows * (east_rims[..., :-2] - east_rims[..., 2:])
    column_force = -zonal_diff[0] - merid_diff[0]
    running = jnp.cumsum(column_force, axis=0)
    carried = entering(
        jnp.sum(column_force, axis=0), "lev", jnp.add, jnp.zeros((lat_rows, lon_cells), jnp.float32)
    )
    new_height = adjoint[0] + layer_weight[:, None, None] * (running + carried[None])
    new_east = adjoint[1] - zonal_diff[1] - coriolis_rows * q_north
    new_north = adjoint[2] - merid_diff[1] + coriolis_rows * q_east
    return jnp.stack([new_height, new_east, new_north])


REMOTE = 28
OWN = 28
OTHER = 30
FAR = 32
CODES = 80
PART = 8
GROUP = 2
TILE = 256
LANES = 128
ROWS = 8
ORDER = (2, 0, 1)
MESH = pl.DeviceIdType.MESH


def halves(value):
    high = value.astype(jnp.bfloat16)
    return high, (value - high.astype(jnp.float32)).astype(jnp.bfloat16)


def split_table(value):
    high = np.asarray(value, np.float32).astype(ml_dtypes.bfloat16)
    low = (np.asarray(value, np.float32) - high.astype(np.float32)).astype(ml_dtypes.bfloat16)
    return high, low


def factors(matrix, rank):
    u, s, v = np.linalg.svd(matrix, full_matrices=False)
    size = np.sqrt(s[:rank])
    return u[:, :rank] * size, v[:rank].T * size


@functools.lru_cache(maxsize=None)
def kernel_tables(cells):
    circle = 2 * cells

    def kernel(distance):
        wave = circle * np.sin(np.pi * (distance % (2 * circle)) / circle)
        return np.where(distance % circle == 0, 0.0, 1.0 / np.where(distance % circle == 0, 1.0, wave))

    n = np.arange(cells)
    here = kernel(n[:, None] - n[None, :])
    project = np.zeros((cells, LANES))
    expand = np.zeros((LANES, cells))
    left, right = factors(kernel(n[:, None] - n[None, :] - cells), REMOTE)
    project[:, :REMOTE] = right
    expand[:REMOTE] = left.T
    project[:, OWN] = kernel(cells - 1 - n)
    project[:, OWN + 1] = kernel(0 - n)
    project[:, OTHER] = kernel(cells - 1 - n - cells)
    project[:, OTHER + 1] = kernel(0 - n - cells)
    blocks = cells // TILE
    at = FAR
    for block in range(blocks):
        part = slice(block * TILE, (block + 1) * TILE)
        far = here[part].copy()
        far[:, part] = 0.0
        rank = 12 if block in (0, blocks - 1) else 18
        left, right = factors(far, rank)
        project[:, at : at + rank] = right
        expand[at : at + rank, part] = left.T
        at += rank
    split = cells // 2
    turned = np.roll(expand, 48, axis=0)
    groups = []
    for part in (expand[:CODES, :split], turned[:CODES, split:]):
        high, low = split_table(part)
        groups.append(np.concatenate([high, high, low, np.zeros((TILE - 3 * CODES, split), high.dtype)]))
    near = kernel(n[:TILE, None] - n[None, :TILE]).T
    project_high, project_low = split_table(project)
    near_high, near_low = split_table(near)
    return (
        np.concatenate([project_high, project_low], axis=1),
        np.concatenate(groups, axis=1),
        np.concatenate([near_high, near_high, near_low]),
    )


def column(ref, first, kind=jnp.float32):
    row = lax.broadcasted_iota(jnp.int32, (ROWS, LANES), 0)
    value = jnp.zeros((ROWS, LANES), kind)
    for turn in range(ROWS):
        value = jnp.where(row == turn, ref[first + turn], value)
    return value


def across(value, width):
    return jnp.concatenate([value] * (width // LANES), axis=1)


def filter_kernel(
    merid_hbm, cuts_hbm, flags_hbm, zonal_hbm, coriolis_hbm, weight_hbm, x_hbm, depth_hbm, project_hbm, expand_hbm, near_hbm,
    out_ref, edges_ref,
    merid_ref, cuts_ref, flags_ref, zonal_ref, coriolis_ref, weight_ref, q_ref, rims_ref, x_ref, depth_ref,
    project_ref, expand_ref, near_ref, high_ref, low_ref, code_ref, edge_ref, send_ref, take_ref,
    rows_ref, brink_ref, scalar_sem, load_sem, table_sem, out_sem, in_sem, leave_sem, reach_sem,
):
    fields, levels, rows, cells = x_ref.shape
    circle = 2 * cells
    count = levels * rows
    half = count // 2
    lat_count = lax.axis_size("lat")
    lat = lax.axis_index("lat")
    lon = lax.axis_index("lon")
    scalars = [
        pltpu.make_async_copy(source, target, scalar_sem.at[turn])
        for turn, (source, target) in enumerate(
            (
                (cuts_hbm, cuts_ref), (flags_hbm, flags_ref), (merid_hbm, merid_ref),
                (zonal_hbm, zonal_ref), (coriolis_hbm, coriolis_ref), (weight_hbm, weight_ref),
            )
        )
    ]
    for scalar in scalars:
        scalar.start()
    loads = [pltpu.make_async_copy(x_hbm.at[f], x_ref.at[f], load_sem.at[f]) for f in range(fields)]
    tables = [
        pltpu.make_async_copy(source, target, table_sem.at[turn])
        for turn, (source, target) in enumerate(
            ((project_hbm, project_ref), (depth_hbm, depth_ref), (near_hbm, near_ref), (expand_hbm, expand_ref))
        )
    ]
    loads[ORDER[0]].start()
    tables[0].start()
    loads[ORDER[1]].start()
    tables[1].start()
    loads[ORDER[2]].start()
    tables[2].start()
    tables[3].start()

    barrier = pltpu.get_barrier_semaphore()
    pl.semaphore_signal(barrier, inc=1, device_id={"lon": 1 - lon}, device_id_type=MESH)

    up = {"lat": jnp.minimum(lat + 1, lat_count - 1), "lon": jnp.where(lat < lat_count - 1, lon, 1 - lon)}
    down = {"lat": jnp.maximum(lat - 1, 0), "lon": jnp.where(lat > 0, lon, 1 - lon)}
    upward = [lat % 2, 1 - lat % 2]
    targets = [{name: jnp.where(way == 1, up[name], down[name]) for name in up} for way in upward]
    slots = [
        jnp.where(way == 1, jnp.where(lat < lat_count - 1, 0, 1), jnp.where(lat > 0, 1, 0)) for way in upward
    ]
    for target in targets:
        pl.semaphore_signal(barrier, inc=1, device_id=target, device_id_type=MESH)

    for scalar in scalars:
        scalar.wait()
    first = lat * rows
    cuts = column(cuts_ref, first, jnp.int32)
    on = jnp.where(column(flags_ref, first, jnp.int32) > 0, 1.0, 0.0)
    at_end = jnp.where(lat == 0, 0, jnp.where(lat == lat_count - 1, rows - 1, -1))
    row = lax.broadcasted_iota(jnp.int32, (rows, LANES), 0)
    merid = column(merid_ref, first)
    zonal = column(zonal_ref, first)
    coriolis = column(coriolis_ref, first)
    brink = jnp.where(row == at_end, 0.0, merid)
    kept = (2 * cuts + 1).astype(jnp.float32)
    keep = jnp.where(on > 0.0, kept * (1.0 / circle), 1.0)
    odd = jnp.bitwise_and(cuts, 1)
    sign = on * jnp.where(odd == 0, -1.0, 1.0)
    place = lax.broadcasted_iota(jnp.int32, (rows, cells), 1).astype(jnp.float32)
    phase = across(kept, cells) * place
    phase = phase - jnp.floor(phase * (1.0 / (2 * circle))) * (2.0 * circle)
    angle = phase * (math.pi / circle)
    cos = across(on, cells) * jnp.cos(angle)
    sin = across(on, cells) * jnp.sin(angle)
    lane = lax.broadcasted_iota(jnp.int32, (rows, LANES), 1)

    def at_edges(end, start, low):
        return jnp.where(lane == low, end, jnp.where(lane == low + 1, start, 0.0))

    end_cos, end_sin = cos[:, cells - 1 :], sin[:, cells - 1 :]
    start_cos, start_sin = cos[:, :1], sin[:, :1]
    mix_cos = at_edges(end_sin, start_sin, OWN) + at_edges(sign * end_cos, sign * start_cos, OTHER)
    mix_sin = at_edges(-end_cos, -start_cos, OWN) + at_edges(sign * end_sin, sign * start_sin, OTHER)
    rows_ref[0] = cos
    rows_ref[1] = sin

    def exchange(field):
        return pltpu.make_async_remote_copy(
            src_ref=send_ref.at[field], dst_ref=take_ref.at[field], send_sem=out_sem.at[field],
            recv_sem=in_sem.at[field], device_id={"lon": 1 - lon}, device_id_type=MESH,
        )

    def spread(value):
        return jnp.broadcast_to(value[None], (levels,) + value.shape).reshape(count, value.shape[1])

    groups = cells // TILE // GROUP

    def send(turn, which, group, slot):
        at = pl.ds(group * GROUP * TILE, GROUP * TILE)
        place = which * groups + group
        return pltpu.make_async_remote_copy(
            src_ref=brink_ref.at[upward[turn], which, :, at], dst_ref=edges_ref.at[slot, which, :, at],
            send_sem=leave_sem.at[turn, place], recv_sem=reach_sem.at[slot, place],
            device_id=targets[turn], device_id_type=MESH,
        )

    lane_all = lax.broadcasted_iota(jnp.int32, (count, LANES), 1)
    part = 8
    for turn, field in enumerate(ORDER):
        loads[field].wait()
        for group in range(levels // part):
            x = x_ref[field, group * part : (group + 1) * part]
            for which in range(2):
                high, low = halves((x * rows_ref[which][None]).reshape(part * rows, cells))
                at = slice(which * count + group * part * rows, which * count + (group + 1) * part * rows)
                high_ref[field, at] = high
                low_ref[field, at] = low
        if turn == 0:
            tables[0].wait()
        table = project_ref[...]
        total = jnp.dot(high_ref[field], table, preferred_element_type=jnp.float32)
        total = total + jnp.dot(low_ref[field], table, preferred_element_type=jnp.float32)
        code = total[:, :LANES] + total[:, LANES:]
        code_ref[field] = code
        code_cos, code_sin = code[:count], code[count:]
        message = jnp.where(lane_all < 32, code_cos, pltpu.roll(code_sin, 32, 1))
        if field < 2:
            edge = spread(mix_cos) * code_cos + spread(mix_sin) * code_sin
            start, end = x_ref[field, :, :, :LANES], x_ref[field, :, :, cells - LANES :]
            start, end = start.reshape(count, LANES)[:, :1], end.reshape(count, LANES)[:, LANES - 1 :]
            edge = edge + spread(keep) * jnp.where(lane_all == OWN, end, jnp.where(lane_all == OWN + 1, start, 0.0))
            edge_ref[field] = edge
            message = jnp.where(jnp.logical_and(lane_all >= OWN, lane_all < OWN + 2), edge, message)
        if field == 0:
            tables[1].wait()
            start, end = depth_ref[:, :, :LANES], depth_ref[:, :, cells - LANES :]
            start = start.astype(jnp.float32).reshape(count, LANES)[:, :1]
            end = end.astype(jnp.float32).reshape(count, LANES)[:, LANES - 1 :]
            message = jnp.where(lane_all == OWN + 32, end, jnp.where(lane_all == OWN + 33, start, message))
        send_ref[field] = jnp.where(lane_all[:half] < 64, message[:half], pltpu.roll(message[half:], 64, 1))
        if turn == 0:
            pl.semaphore_wait(barrier, 3)
        exchange(field).start()

    tables[2].wait()
    tables[3].wait()
    lane_row = lax.broadcasted_iota(jnp.int32, (rows, LANES), 1)
    row_all = lax.broadcasted_iota(jnp.int32, (rows, cells), 0)

    def zonal_adjoint(value, rims):
        left, right = pltpu.roll(value, 1, 1), pltpu.roll(value, cells - 1, 1)
        left = jnp.concatenate([jnp.where(lane_row == 0, rims, left[:, :LANES]), left[:, LANES:]], axis=1)
        last = cells - LANES
        right = jnp.concatenate([right[:, :last], jnp.where(lane_row == LANES - 1, rims, right[:, last:])], axis=1)
        return across(zonal, cells) * (left - right)

    def merid_adjoint(value):
        value = across(merid, cells) * value
        up = jnp.where(row_all == 0, 0.0, pltpu.roll(value, 1, 0))
        down = jnp.where(row_all == rows - 1, 0.0, pltpu.roll(value, rows - 1, 0))
        return up - down

    def fluxes(level):
        north = q_ref[2, level]
        flux = depth_ref[level].astype(jnp.float32) * q_ref[0, level]
        out_ref[1, level] = x_ref[1, level] - zonal_adjoint(flux, rims_ref[0, level]) - across(coriolis, cells) * north
        out_ref[2, level] = x_ref[2, level] - merid_adjoint(flux)

    def forces(level, run):
        east = q_ref[1, level]
        run = run - (zonal_adjoint(east, rims_ref[1, level]) + out_ref[0, level])
        out_ref[0, level] = x_ref[0, level] + weight_ref[level] * run
        out_ref[2, level] += across(coriolis, cells) * east
        return run

    for field in ORDER:
        exchange(field).wait_recv()
        taken = take_ref[field]
        taken = jnp.concatenate([taken, pltpu.roll(taken, 64, 1)])
        turned = pltpu.roll(taken, 96, 1)
        if field < 2:
            rims = taken + pltpu.roll(edge_ref[field], LANES - 2, 1)
            if field == 0:
                rims = rims * turned
            rims = jnp.where(
                lane_all == LANES - 1, pltpu.roll(rims, LANES - 2 - OWN, 1), pltpu.roll(rims, LANES - OWN, 1)
            )
            rims_ref[field] = rims.reshape(levels, rows, LANES)
        signs = spread(sign)
        code = code_ref[field]
        code = jnp.concatenate(
            [
                jnp.where(lane_all < REMOTE, signs * turned, code[:count]),
                jnp.where(lane_all < REMOTE, -signs * taken, code[count:]),
            ]
        )
        code_high = code.astype(jnp.bfloat16).astype(jnp.float32)
        code_low = code - code_high
        lane_both = lax.broadcasted_iota(jnp.int32, code.shape, 1)
        packed = []
        for low, head, rest in (
            (pltpu.roll(code_low, CODES, 1), code_high, pltpu.roll(code_high, 32, 1)),
            (code_low, pltpu.roll(code_high, 48, 1), pltpu.roll(code_high, 80, 1)),
        ):
            pair = (jnp.where(lane_both < CODES, head, low), jnp.where(lane_both < 32, low, rest))
            packed.append([value.astype(jnp.bfloat16) for value in pair])
        for block in range(cells // TILE):
            at = slice(block * TILE, (block + 1) * TILE)
            high, low = high_ref[field, :, at], low_ref[field, :, at]
            terms = jnp.concatenate([high, low, high, *packed[2 * at.start // cells]], axis=1)
            weights = jnp.concatenate([near_ref[...], expand_ref[:, at]], axis=0)
            value = jnp.dot(terms, weights, preferred_element_type=jnp.float32)
            shape = (levels, rows, TILE)
            result = across(keep, TILE)[None] * x_ref[field, :, :, at]
            result = result + rows_ref[1, :, at][None] * value[:count].reshape(shape)
            result = result - rows_ref[0, :, at][None] * value[count:].reshape(shape)
            q_ref[field, :, :, at] = result
            turns = range(block * levels * TILE // cells, (block + 1) * levels * TILE // cells)
            for level in turns if field == 0 else ():
                out_ref[0, level] = merid_adjoint(q_ref[2, level])
            for level in turns if field == 1 else ():
                fluxes(level)
            if field != 1:
                edge = result
                if field == 0:
                    edge = result * depth_ref[:, :, at].astype(jnp.float32)
                edge = edge * across(brink, TILE)[None]
                which = 0 if field == 2 else 1
                brink_ref[0, which, :, at] = edge[:, 0, :]
                brink_ref[1, which, :, at] = edge[:, rows - 1, :]
                if block % GROUP == GROUP - 1:
                    for turn in range(2):
                        send(turn, which, block // GROUP, slots[turn]).start()

    def tail(step, run):
        for turn in range(4):
            level = step * 4 + turn
            run = forces(level, run)
        return run

    lax.fori_loop(0, levels // 4, tail, jnp.zeros((rows, cells), jnp.float32))
    for field in ORDER:
        exchange(field).wait_send()

    for which in range(2):
        for group in range(groups):
            for turn in range(2):
                send(turn, which, group, slots[turn]).wait_send()
                send(turn, which, group, turn).wait_recv()


def final_kernel(weight_ref, part_ref, edges_ref, out_hbm, done_ref, sems):
    _, levels, rows, cells = part_ref.shape
    row = lax.broadcasted_iota(jnp.int32, (rows, cells), 0)
    copies = [pltpu.make_async_copy(part_ref.at[1], out_hbm.at[1], sems.at[0])]
    copies[0].start()

    def missing(which, level):
        before, after = edges_ref[0, which, level : level + 1, :], edges_ref[1, which, level : level + 1, :]
        return jnp.where(row == 0, before, jnp.where(row == rows - 1, -after, 0.0))

    run = jnp.zeros((rows, cells), jnp.float32)
    for level in range(levels):
        run = run - missing(0, level)
        done_ref[0, level] = part_ref[0, level] + weight_ref[level] * run
        done_ref[1, level] = part_ref[2, level] - missing(1, level)
        if level % PART == PART - 1:
            at = pl.ds(level - PART + 1, PART)
            for turn, field in enumerate((0, 2)):
                copies.append(
                    pltpu.make_async_copy(done_ref.at[turn, at], out_hbm.at[field, at], sems.at[len(copies)])
                )
                copies[-1].start()
    for copy in copies:
        copy.wait()


def on_pair(adjoint, depth, zonal_coef, merid_coef, coriolis, layer_weight, cutoffs, polar_flags):
    fields, level_count, rows, cells = adjoint.shape
    project, expand, near = (jnp.asarray(table) for table in kernel_tables(cells))
    count = level_count * rows
    pieces = cells // TILE // GROUP
    scalars = pl.BlockSpec(memory_space=pltpu.SMEM)
    there = pl.BlockSpec(memory_space=pltpu.HBM)
    close = pl.BlockSpec(memory_space=pltpu.VMEM)
    single = jnp.float32
    dma = pltpu.SemaphoreType.DMA

    partial, edges = pl.pallas_call(
        filter_kernel,
        in_specs=[there] * 11,
        out_specs=[close] * 2,
        out_shape=[
            jax.ShapeDtypeStruct(adjoint.shape, single),
            jax.ShapeDtypeStruct((2, 2, level_count, cells), single),
        ],
        scratch_shapes=[
            pltpu.SMEM(merid_coef.shape, single),
            pltpu.SMEM(cutoffs.shape, jnp.int32),
            pltpu.SMEM(polar_flags.shape, jnp.int32),
            pltpu.SMEM(zonal_coef.shape, single),
            pltpu.SMEM(coriolis.shape, single),
            pltpu.SMEM(layer_weight.shape, single),
            pltpu.VMEM(adjoint.shape, single),
            pltpu.VMEM((2, level_count, rows, LANES), single),
            pltpu.VMEM(adjoint.shape, single),
            pltpu.VMEM(depth.shape, depth.dtype),
            pltpu.VMEM(project.shape, project.dtype),
            pltpu.VMEM(expand.shape, expand.dtype),
            pltpu.VMEM(near.shape, near.dtype),
            pltpu.VMEM((fields, 2 * count, cells), jnp.bfloat16),
            pltpu.VMEM((fields, 2 * count, cells), jnp.bfloat16),
            pltpu.VMEM((fields, 2 * count, LANES), single),
            pltpu.VMEM((2, count, LANES), single),
            pltpu.VMEM((fields, count // 2, LANES), single),
            pltpu.VMEM((fields, count // 2, LANES), single),
            pltpu.VMEM((2, rows, cells), single),
            pltpu.VMEM((2, 2, level_count, cells), single),
            dma((6,)),
            dma((3,)),
            dma((4,)),
            dma((3,)),
            dma((3,)),
            dma((2, 2 * pieces)),
            dma((2, 2 * pieces)),
        ],
        compiler_params=pltpu.CompilerParams(
            collective_id=0, has_side_effects=True, vmem_limit_bytes=36 * 2**20
        ),
    )(*(pltpu.with_memory_space_constraint(value, pltpu.HBM) for value in (merid_coef, cutoffs, polar_flags, zonal_coef, coriolis, layer_weight, adjoint, depth, project, expand, near)))

    return pl.pallas_call(
        final_kernel,
        in_specs=[scalars] + [close] * 2,
        out_specs=pl.BlockSpec(memory_space=pl.ANY),
        out_shape=jax.ShapeDtypeStruct(adjoint.shape, single),
        scratch_shapes=[pltpu.VMEM((2,) + adjoint.shape[1:], single), dma((1 + 2 * level_count // PART,))],
        compiler_params=pltpu.CompilerParams(vmem_limit_bytes=32 * 2**20),
    )(layer_weight, partial, edges)


def plan_for(mesh):
    return on_pair if mesh.shape["lon"] == 2 and mesh.shape["lev"] == 1 else on_device


def solution(mesh):
    return jax.shard_map(
        plan_for(mesh),
        mesh=mesh,
        in_specs=(
            P("member", "lev", "lat", "lon"),
            P("lev", "lat", "lon"),
            P(),
            P(),
            P(),
            P("lev"),
            P(),
            P(),
        ),
        out_specs=P("member", "lev", "lat", "lon"),
        check_vma=False,
    )
```

```python
import functools
import math

import jax
import jax.numpy as jnp
import ml_dtypes
import numpy as np
from jax import lax
from jax.experimental import pallas as pl
from jax.experimental.pallas import tpu as pltpu
from jax.sharding import PartitionSpec as P

KMAX = 1024
POLE_ROWS = 24


def extended(cells, sides, width, closed):
    for axis, dim in sides:
        count = lax.axis_size(axis)
        ends = count if closed else count - 1
        head = lax.slice_in_dim(cells, 0, width, axis=dim)
        tail = lax.slice_in_dim(cells, cells.shape[dim] - width, cells.shape[dim], axis=dim)
        cells = jnp.concatenate(
            [
                lax.ppermute(tail, axis, [(i, (i + 1) % count) for i in range(ends)]),
                cells,
                lax.ppermute(head, axis, [((i + 1) % count, i) for i in range(ends)]),
            ],
            axis=dim,
        )
    return cells


def entering(value, axis, join, neutral):
    count, mine = (lax.axis_size(axis), lax.axis_index(axis))
    pieces = lax.all_gather(value, axis)
    total = jnp.full_like(value, 0) + jnp.asarray(neutral, value.dtype)

    def turn(position, total):
        longer = join(total, pieces[position])
        return jnp.where(position < mine, longer, total)

    return lax.fori_loop(0, count - 1, turn, total)


def wave_table(col_count, wave_start, wave_count, circle):
    columns = lax.iota(jnp.int32, col_count)
    wave_index = wave_start + lax.iota(jnp.int32, wave_count)
    phase = columns[:, None] * wave_index[None, :] % circle
    angle = phase.astype(jnp.float32) * (2.0 * math.pi / circle)
    return jnp.concatenate([jnp.cos(angle), jnp.sin(angle)], axis=1)


def keep_weights(cut_rows, wave_start, wave_count, circle):
    wave_index = wave_start + lax.iota(jnp.int32, wave_count)
    factor = jnp.where(wave_index == 0, 1.0, 2.0) / circle
    kept = (wave_index[None, :] <= cut_rows[:, None]).astype(jnp.float32) * factor[None, :]
    return jnp.concatenate([kept, kept], axis=1)


def block_width():
    return min(KMAX, 128)


def project_rows(row_data, cut_rows):
    circle = row_data.shape[1]
    width = block_width()
    result = jnp.zeros(row_data.shape, jnp.float32)
    for block_index in range(KMAX // width):
        table = wave_table(circle, block_index * width, width, circle)
        coefs = jnp.dot(
            row_data, table, precision=lax.Precision.HIGHEST, preferred_element_type=jnp.float32
        )
        weights = keep_weights(cut_rows, block_index * width, width, circle)
        result = result + jnp.dot(
            coefs * weights,
            table.T,
            precision=lax.Precision.HIGHEST,
            preferred_element_type=jnp.float32,
        )
    return result


def transpose_filter(row_data, cut_rows, flag_rows):
    lon_count = lax.axis_size("lon")
    lon_index = lax.axis_index("lon")
    share = row_data.shape[0] // lon_count
    full_rows = lax.all_to_all(row_data, "lon", split_axis=0, concat_axis=1, tiled=True)
    my_cuts = lax.dynamic_slice_in_dim(cut_rows, lon_index * share, share)
    smoothed = project_rows(full_rows, my_cuts)
    returned = lax.all_to_all(smoothed, "lon", split_axis=1, concat_axis=0, tiled=True)
    return jnp.where(flag_rows[:, None] > 0, returned, row_data)


def polar_filter(row_data, cut_rows, flag_rows):
    return transpose_filter(row_data, cut_rows, flag_rows)


def on_device(adjoint, depth, zonal_coef, merid_coef, coriolis, layer_weight, cutoffs, polar_flags):
    fields, level_count, lat_rows, lon_cells = adjoint.shape
    lat_index = lax.axis_index("lat")
    lat_total = lat_rows * lax.axis_size("lat")
    stacked = adjoint.reshape(fields * level_count, lat_rows, lon_cells)
    bands = lax.all_to_all(stacked, "lat", split_axis=0, concat_axis=1, tiled=True)
    groups = bands.shape[0]
    polar_block = jnp.concatenate([bands[:, :POLE_ROWS], bands[:, lat_total - POLE_ROWS :]], axis=1)
    polar_cuts = jnp.concatenate([cutoffs[:POLE_ROWS], cutoffs[lat_total - POLE_ROWS :]])
    polar_marks = jnp.concatenate([polar_flags[:POLE_ROWS], polar_flags[lat_total - POLE_ROWS :]])
    row_data = polar_block.reshape(groups * 2 * POLE_ROWS, lon_cells)
    cut_rows = jnp.tile(polar_cuts, groups)
    flag_rows = jnp.tile(polar_marks, groups)
    treated = polar_filter(row_data, cut_rows, flag_rows)
    treated = treated.reshape(groups, 2 * POLE_ROWS, lon_cells)
    bands = jnp.concatenate(
        [
            treated[:, :POLE_ROWS],
            bands[:, POLE_ROWS : lat_total - POLE_ROWS],
            treated[:, POLE_ROWS:],
        ],
        axis=1,
    )
    filtered = lax.all_to_all(bands, "lat", split_axis=1, concat_axis=0, tiled=True).reshape(
        adjoint.shape
    )
    q_height = filtered[0]
    q_east = filtered[1]
    q_north = filtered[2]
    zonal_rows = lax.dynamic_slice_in_dim(zonal_coef, lat_index * lat_rows, lat_rows)[None, :, None]
    merid_rows = lax.dynamic_slice_in_dim(merid_coef, lat_index * lat_rows, lat_rows)[None, :, None]
    coriolis_rows = lax.dynamic_slice_in_dim(coriolis, lat_index * lat_rows, lat_rows)[
        None, :, None
    ]
    height_flux = depth.astype(jnp.float32) * q_height
    north_pair = jnp.stack([merid_rows * q_north, merid_rows * height_flux])
    north_rims = extended(north_pair, (("lat", 2),), 1, False)
    merid_diff = north_rims[:, :, :-2] - north_rims[:, :, 2:]
    east_pair = jnp.stack([q_east, height_flux])
    east_rims = extended(east_pair, (("lon", 3),), 1, True)
    zonal_diff = zonal_rows * (east_rims[..., :-2] - east_rims[..., 2:])
    column_force = -zonal_diff[0] - merid_diff[0]
    running = jnp.cumsum(column_force, axis=0)
    carried = entering(
        jnp.sum(column_force, axis=0), "lev", jnp.add, jnp.zeros((lat_rows, lon_cells), jnp.float32)
    )
    new_height = adjoint[0] + layer_weight[:, None, None] * (running + carried[None])
    new_east = adjoint[1] - zonal_diff[1] - coriolis_rows * q_north
    new_north = adjoint[2] - merid_diff[1] + coriolis_rows * q_east
    return jnp.stack([new_height, new_east, new_north])


REMOTE = 28
OWN = 28
OTHER = 30
FAR = 32
CODES = 80
PART = 8
GROUP = 2
TILE = 256
LANES = 128
ROWS = 8
ORDER = (2, 0, 1)
MESH = pl.DeviceIdType.MESH


def halves(value):
    high = value.astype(jnp.bfloat16)
    return high, (value - high.astype(jnp.float32)).astype(jnp.bfloat16)


def split_table(value):
    high = np.asarray(value, np.float32).astype(ml_dtypes.bfloat16)
    low = (np.asarray(value, np.float32) - high.astype(np.float32)).astype(ml_dtypes.bfloat16)
    return high, low


def factors(matrix, rank):
    u, s, v = np.linalg.svd(matrix, full_matrices=False)
    size = np.sqrt(s[:rank])
    return u[:, :rank] * size, v[:rank].T * size


@functools.lru_cache(maxsize=None)
def kernel_tables(cells):
    circle = 2 * cells

    def kernel(distance):
        wave = circle * np.sin(np.pi * (distance % (2 * circle)) / circle)
        return np.where(distance % circle == 0, 0.0, 1.0 / np.where(distance % circle == 0, 1.0, wave))

    n = np.arange(cells)
    here = kernel(n[:, None] - n[None, :])
    project = np.zeros((cells, LANES))
    expand = np.zeros((LANES, cells))
    left, right = factors(kernel(n[:, None] - n[None, :] - cells), REMOTE)
    project[:, :REMOTE] = right
    expand[:REMOTE] = left.T
    project[:, OWN] = kernel(cells - 1 - n)
    project[:, OWN + 1] = kernel(0 - n)
    project[:, OTHER] = kernel(cells - 1 - n - cells)
    project[:, OTHER + 1] = kernel(0 - n - cells)
    blocks = cells // TILE
    at = FAR
    for block in range(blocks):
        part = slice(block * TILE, (block + 1) * TILE)
        far = here[part].copy()
        far[:, part] = 0.0
        rank = 12 if block in (0, blocks - 1) else 18
        left, right = factors(far, rank)
        project[:, at : at + rank] = right
        expand[at : at + rank, part] = left.T
        at += rank
    split = cells // 2
    turned = np.roll(expand, 48, axis=0)
    groups = []
    for part in (expand[:CODES, :split], turned[:CODES, split:]):
        high, low = split_table(part)
        groups.append(np.concatenate([high, high, low, np.zeros((TILE - 3 * CODES, split), high.dtype)]))
    near = kernel(n[:TILE, None] - n[None, :TILE]).T
    project_high, project_low = split_table(project)
    near_high, near_low = split_table(near)
    return (
        np.concatenate([project_high, project_low], axis=1),
        np.concatenate(groups, axis=1),
        np.concatenate([near_high, near_high, near_low]),
    )


def column(ref, first, kind=jnp.float32):
    row = lax.broadcasted_iota(jnp.int32, (ROWS, LANES), 0)
    value = jnp.zeros((ROWS, LANES), kind)
    for turn in range(ROWS):
        value = jnp.where(row == turn, ref[first + turn], value)
    return value


def across(value, width):
    return jnp.concatenate([value] * (width // LANES), axis=1)


def filter_kernel(
    merid_hbm, cuts_hbm, flags_hbm, zonal_hbm, coriolis_hbm, weight_hbm, x_hbm, depth_hbm, project_hbm, expand_hbm, near_hbm,
    out_ref, edges_ref,
    merid_ref, cuts_ref, flags_ref, zonal_ref, coriolis_ref, weight_ref, q_ref, rims_ref, x_ref, depth_ref,
    project_ref, expand_ref, near_ref, high_ref, low_ref, code_ref, edge_ref, send_ref, take_ref,
    rows_ref, brink_ref, scalar_sem, load_sem, table_sem, out_sem, in_sem, leave_sem, reach_sem,
):
    fields, levels, rows, cells = x_ref.shape
    circle = 2 * cells
    count = levels * rows
    half = count // 2
    lat_count = lax.axis_size("lat")
    lat = lax.axis_index("lat")
    lon = lax.axis_index("lon")
    scalars = [
        pltpu.make_async_copy(source, target, scalar_sem.at[turn])
        for turn, (source, target) in enumerate(
            (
                (cuts_hbm, cuts_ref), (flags_hbm, flags_ref), (merid_hbm, merid_ref),
                (zonal_hbm, zonal_ref), (coriolis_hbm, coriolis_ref), (weight_hbm, weight_ref),
            )
        )
    ]
    for scalar in scalars:
        scalar.start()
    loads = {f: pltpu.make_async_copy(x_hbm.at[f], x_ref.at[f], load_sem.at[f]) for f in ORDER[1:]}
    quarters = [
        pltpu.make_async_copy(
            x_hbm.at[ORDER[0], pl.ds(start, 8)], x_ref.at[ORDER[0], pl.ds(start, 8)], load_sem.at[fields + start // 8]
        )
        for start in range(0, levels, 8)
    ]
    tables = [
        pltpu.make_async_copy(source, target, table_sem.at[turn])
        for turn, (source, target) in enumerate(
            ((project_hbm, project_ref), (depth_hbm, depth_ref), (near_hbm, near_ref), (expand_hbm, expand_ref))
        )
    ]
    for quarter in quarters:
        quarter.start()
    tables[0].start()
    loads[ORDER[1]].start()
    tables[1].start()
    loads[ORDER[2]].start()
    tables[2].start()
    tables[3].start()

    barrier = pltpu.get_barrier_semaphore()
    pl.semaphore_signal(barrier, inc=1, device_id={"lon": 1 - lon}, device_id_type=MESH)

    up = {"lat": jnp.minimum(lat + 1, lat_count - 1), "lon": jnp.where(lat < lat_count - 1, lon, 1 - lon)}
    down = {"lat": jnp.maximum(lat - 1, 0), "lon": jnp.where(lat > 0, lon, 1 - lon)}
    upward = [lat % 2, 1 - lat % 2]
    targets = [{name: jnp.where(way == 1, up[name], down[name]) for name in up} for way in upward]
    slots = [
        jnp.where(way == 1, jnp.where(lat < lat_count - 1, 0, 1), jnp.where(lat > 0, 1, 0)) for way in upward
    ]
    for target in targets:
        pl.semaphore_signal(barrier, inc=1, device_id=target, device_id_type=MESH)

    for scalar in scalars:
        scalar.wait()
    first = lat * rows
    cuts = column(cuts_ref, first, jnp.int32)
    on = jnp.where(column(flags_ref, first, jnp.int32) > 0, 1.0, 0.0)
    at_end = jnp.where(lat == 0, 0, jnp.where(lat == lat_count - 1, rows - 1, -1))
    row = lax.broadcasted_iota(jnp.int32, (rows, LANES), 0)
    merid = column(merid_ref, first)
    zonal = column(zonal_ref, first)
    coriolis = column(coriolis_ref, first)
    brink = jnp.where(row == at_end, 0.0, merid)
    kept = (2 * cuts + 1).astype(jnp.float32)
    keep = jnp.where(on > 0.0, kept * (1.0 / circle), 1.0)
    odd = jnp.bitwise_and(cuts, 1)
    sign = on * jnp.where(odd == 0, -1.0, 1.0)
    place = lax.broadcasted_iota(jnp.int32, (rows, cells), 1).astype(jnp.float32)
    phase = across(kept, cells) * place
    phase = phase - jnp.floor(phase * (1.0 / (2 * circle))) * (2.0 * circle)
    angle = phase * (math.pi / circle)
    cos = across(on, cells) * jnp.cos(angle)
    sin = across(on, cells) * jnp.sin(angle)
    lane = lax.broadcasted_iota(jnp.int32, (rows, LANES), 1)

    def at_edges(end, start, low):
        return jnp.where(lane == low, end, jnp.where(lane == low + 1, start, 0.0))

    end_cos, end_sin = cos[:, cells - 1 :], sin[:, cells - 1 :]
    start_cos, start_sin = cos[:, :1], sin[:, :1]
    mix_cos = at_edges(end_sin, start_sin, OWN) + at_edges(sign * end_cos, sign * start_cos, OTHER)
    mix_sin = at_edges(-end_cos, -start_cos, OWN) + at_edges(sign * end_sin, sign * start_sin, OTHER)
    rows_ref[0] = cos
    rows_ref[1] = sin

    def exchange(field):
        return pltpu.make_async_remote_copy(
            src_ref=send_ref.at[field], dst_ref=take_ref.at[field], send_sem=out_sem.at[field],
            recv_sem=in_sem.at[field], device_id={"lon": 1 - lon}, device_id_type=MESH,
        )

    def spread(value):
        return jnp.broadcast_to(value[None], (levels,) + value.shape).reshape(count, value.shape[1])

    groups = cells // TILE // GROUP

    def send(turn, which, group, slot):
        at = pl.ds(group * GROUP * TILE, GROUP * TILE)
        place = which * groups + group
        return pltpu.make_async_remote_copy(
            src_ref=brink_ref.at[upward[turn], which, :, at], dst_ref=edges_ref.at[slot, which, :, at],
            send_sem=leave_sem.at[turn, place], recv_sem=reach_sem.at[slot, place],
            device_id=targets[turn], device_id_type=MESH,
        )

    lane_all = lax.broadcasted_iota(jnp.int32, (count, LANES), 1)
    part = 8
    for turn, field in enumerate(ORDER):
        if field != ORDER[0]:
            loads[field].wait()
        for group in range(levels // part):
            if field == ORDER[0]:
                quarters[group].wait()
            x = x_ref[field, group * part : (group + 1) * part]
            for which in range(2):
                high, low = halves((x * rows_ref[which][None]).reshape(part * rows, cells))
                at = slice(which * count + group * part * rows, which * count + (group + 1) * part * rows)
                high_ref[field, at] = high
                low_ref[field, at] = low
        if turn == 0:
            tables[0].wait()
        table = project_ref[...]
        total = jnp.dot(high_ref[field], table, preferred_element_type=jnp.float32)
        total = total + jnp.dot(low_ref[field], table, preferred_element_type=jnp.float32)
        code = total[:, :LANES] + total[:, LANES:]
        code_ref[field] = code
        code_cos, code_sin = code[:count], code[count:]
        message = jnp.where(lane_all < 32, code_cos, pltpu.roll(code_sin, 32, 1))
        if field < 2:
            edge = spread(mix_cos) * code_cos + spread(mix_sin) * code_sin
            start, end = x_ref[field, :, :, :LANES], x_ref[field, :, :, cells - LANES :]
            start, end = start.reshape(count, LANES)[:, :1], end.reshape(count, LANES)[:, LANES - 1 :]
            edge = edge + spread(keep) * jnp.where(lane_all == OWN, end, jnp.where(lane_all == OWN + 1, start, 0.0))
            edge_ref[field] = edge
            message = jnp.where(jnp.logical_and(lane_all >= OWN, lane_all < OWN + 2), edge, message)
        if field == 0:
            tables[1].wait()
            start, end = depth_ref[:, :, :LANES], depth_ref[:, :, cells - LANES :]
            start = start.astype(jnp.float32).reshape(count, LANES)[:, :1]
            end = end.astype(jnp.float32).reshape(count, LANES)[:, LANES - 1 :]
            message = jnp.where(lane_all == OWN + 32, end, jnp.where(lane_all == OWN + 33, start, message))
        send_ref[field] = jnp.where(lane_all[:half] < 64, message[:half], pltpu.roll(message[half:], 64, 1))
        if turn == 0:
            pl.semaphore_wait(barrier, 3)
        exchange(field).start()

    tables[2].wait()
    tables[3].wait()
    lane_row = lax.broadcasted_iota(jnp.int32, (rows, LANES), 1)
    row_all = lax.broadcasted_iota(jnp.int32, (rows, cells), 0)

    def zonal_adjoint(value, rims):
        left, right = pltpu.roll(value, 1, 1), pltpu.roll(value, cells - 1, 1)
        left = jnp.concatenate([jnp.where(lane_row == 0, rims, left[:, :LANES]), left[:, LANES:]], axis=1)
        last = cells - LANES
        right = jnp.concatenate([right[:, :last], jnp.where(lane_row == LANES - 1, rims, right[:, last:])], axis=1)
        return across(zonal, cells) * (left - right)

    def merid_adjoint(value):
        value = across(merid, cells) * value
        up = jnp.where(row_all == 0, 0.0, pltpu.roll(value, 1, 0))
        down = jnp.where(row_all == rows - 1, 0.0, pltpu.roll(value, rows - 1, 0))
        return up - down

    def fluxes(level):
        north = q_ref[2, level]
        flux = depth_ref[level].astype(jnp.float32) * q_ref[0, level]
        out_ref[1, level] = x_ref[1, level] - zonal_adjoint(flux, rims_ref[0, level]) - across(coriolis, cells) * north
        out_ref[2, level] = x_ref[2, level] - merid_adjoint(flux)

    def forces(level, run):
        east = q_ref[1, level]
        run = run - (zonal_adjoint(east, rims_ref[1, level]) + merid_adjoint(q_ref[2, level]))
        out_ref[0, level] = x_ref[0, level] + weight_ref[level] * run
        out_ref[2, level] += across(coriolis, cells) * east
        return run

    for field in ORDER:
        exchange(field).wait_recv()
        taken = take_ref[field]
        taken = jnp.concatenate([taken, pltpu.roll(taken, 64, 1)])
        turned = pltpu.roll(taken, 96, 1)
        if field < 2:
            rims = taken + pltpu.roll(edge_ref[field], LANES - 2, 1)
            if field == 0:
                rims = rims * turned
            rims = jnp.where(
                lane_all == LANES - 1, pltpu.roll(rims, LANES - 2 - OWN, 1), pltpu.roll(rims, LANES - OWN, 1)
            )
            rims_ref[field] = rims.reshape(levels, rows, LANES)
        signs = spread(sign)
        code = code_ref[field]
        code = jnp.concatenate(
            [
                jnp.where(lane_all < REMOTE, signs * turned, code[:count]),
                jnp.where(lane_all < REMOTE, -signs * taken, code[count:]),
            ]
        )
        code_high = code.astype(jnp.bfloat16).astype(jnp.float32)
        code_low = code - code_high
        lane_both = lax.broadcasted_iota(jnp.int32, code.shape, 1)
        packed = []
        for low, head, rest in (
            (pltpu.roll(code_low, CODES, 1), code_high, pltpu.roll(code_high, 32, 1)),
            (code_low, pltpu.roll(code_high, 48, 1), pltpu.roll(code_high, 80, 1)),
        ):
            pair = (jnp.where(lane_both < CODES, head, low), jnp.where(lane_both < 32, low, rest))
            packed.append([value.astype(jnp.bfloat16) for value in pair])
        for block in range(cells // TILE):
            at = slice(block * TILE, (block + 1) * TILE)
            high, low = high_ref[field, :, at], low_ref[field, :, at]
            terms = jnp.concatenate([high, low, high, *packed[2 * at.start // cells]], axis=1)
            weights = jnp.concatenate([near_ref[...], expand_ref[:, at]], axis=0)
            value = jnp.dot(terms, weights, preferred_element_type=jnp.float32)
            shape = (levels, rows, TILE)
            result = across(keep, TILE)[None] * x_ref[field, :, :, at]
            result = result + rows_ref[1, :, at][None] * value[:count].reshape(shape)
            result = result - rows_ref[0, :, at][None] * value[count:].reshape(shape)
            q_ref[field, :, :, at] = result
            turns = range(block * levels * TILE // cells, (block + 1) * levels * TILE // cells)
            for level in turns if field == 1 else ():
                fluxes(level)
            if field != 1:
                edge = result
                if field == 0:
                    edge = result * depth_ref[:, :, at].astype(jnp.float32)
                edge = edge * across(brink, TILE)[None]
                which = 0 if field == 2 else 1
                brink_ref[0, which, :, at] = edge[:, 0, :]
                brink_ref[1, which, :, at] = edge[:, rows - 1, :]
                if block % GROUP == GROUP - 1:
                    for turn in range(2):
                        send(turn, which, block // GROUP, slots[turn]).start()

    def tail(step, run):
        for turn in range(4):
            level = step * 4 + turn
            run = forces(level, run)
        return run

    lax.fori_loop(0, levels // 4, tail, jnp.zeros((rows, cells), jnp.float32))
    for field in ORDER:
        exchange(field).wait_send()

    for which in range(2):
        for group in range(groups):
            for turn in range(2):
                send(turn, which, group, slots[turn]).wait_send()
                send(turn, which, group, turn).wait_recv()


def final_kernel(weight_ref, part_ref, edges_ref, out_hbm, done_ref, sems):
    _, levels, rows, cells = part_ref.shape
    row = lax.broadcasted_iota(jnp.int32, (rows, cells), 0)
    copies = [pltpu.make_async_copy(part_ref.at[1], out_hbm.at[1], sems.at[0])]
    copies[0].start()

    def missing(which, level):
        before, after = edges_ref[0, which, level : level + 1, :], edges_ref[1, which, level : level + 1, :]
        return jnp.where(row == 0, before, jnp.where(row == rows - 1, -after, 0.0))

    run = jnp.zeros((rows, cells), jnp.float32)
    for level in range(levels):
        run = run - missing(0, level)
        done_ref[0, level] = part_ref[0, level] + weight_ref[level] * run
        done_ref[1, level] = part_ref[2, level] - missing(1, level)
        if level % PART == PART - 1:
            at = pl.ds(level - PART + 1, PART)
            for turn, field in enumerate((0, 2)):
                copies.append(
                    pltpu.make_async_copy(done_ref.at[turn, at], out_hbm.at[field, at], sems.at[len(copies)])
                )
                copies[-1].start()
    for copy in copies:
        copy.wait()


def on_pair(adjoint, depth, zonal_coef, merid_coef, coriolis, layer_weight, cutoffs, polar_flags):
    fields, level_count, rows, cells = adjoint.shape
    project, expand, near = (jnp.asarray(table) for table in kernel_tables(cells))
    count = level_count * rows
    pieces = cells // TILE // GROUP
    scalars = pl.BlockSpec(memory_space=pltpu.SMEM)
    there = pl.BlockSpec(memory_space=pltpu.HBM)
    close = pl.BlockSpec(memory_space=pltpu.VMEM)
    single = jnp.float32
    dma = pltpu.SemaphoreType.DMA

    partial, edges = pl.pallas_call(
        filter_kernel,
        in_specs=[there] * 11,
        out_specs=[close] * 2,
        out_shape=[
            jax.ShapeDtypeStruct(adjoint.shape, single),
            jax.ShapeDtypeStruct((2, 2, level_count, cells), single),
        ],
        scratch_shapes=[
            pltpu.SMEM(merid_coef.shape, single),
            pltpu.SMEM(cutoffs.shape, jnp.int32),
            pltpu.SMEM(polar_flags.shape, jnp.int32),
            pltpu.SMEM(zonal_coef.shape, single),
            pltpu.SMEM(coriolis.shape, single),
            pltpu.SMEM(layer_weight.shape, single),
            pltpu.VMEM(adjoint.shape, single),
            pltpu.VMEM((2, level_count, rows, LANES), single),
            pltpu.VMEM(adjoint.shape, single),
            pltpu.VMEM(depth.shape, depth.dtype),
            pltpu.VMEM(project.shape, project.dtype),
            pltpu.VMEM(expand.shape, expand.dtype),
            pltpu.VMEM(near.shape, near.dtype),
            pltpu.VMEM((fields, 2 * count, cells), jnp.bfloat16),
            pltpu.VMEM((fields, 2 * count, cells), jnp.bfloat16),
            pltpu.VMEM((fields, 2 * count, LANES), single),
            pltpu.VMEM((2, count, LANES), single),
            pltpu.VMEM((fields, count // 2, LANES), single),
            pltpu.VMEM((fields, count // 2, LANES), single),
            pltpu.VMEM((2, rows, cells), single),
            pltpu.VMEM((2, 2, level_count, cells), single),
            dma((6,)),
            dma((3 + level_count // 8,)),
            dma((4,)),
            dma((3,)),
            dma((3,)),
            dma((2, 2 * pieces)),
            dma((2, 2 * pieces)),
        ],
        compiler_params=pltpu.CompilerParams(
            collective_id=0, has_side_effects=True, vmem_limit_bytes=36 * 2**20
        ),
    )(*(pltpu.with_memory_space_constraint(value, pltpu.HBM) for value in (merid_coef, cutoffs, polar_flags, zonal_coef, coriolis, layer_weight, adjoint, depth, project, expand, near)))

    return pl.pallas_call(
        final_kernel,
        in_specs=[scalars] + [close] * 2,
        out_specs=pl.BlockSpec(memory_space=pl.ANY),
        out_shape=jax.ShapeDtypeStruct(adjoint.shape, single),
        scratch_shapes=[pltpu.VMEM((2,) + adjoint.shape[1:], single), dma((1 + 2 * level_count // PART,))],
        compiler_params=pltpu.CompilerParams(vmem_limit_bytes=32 * 2**20),
    )(layer_weight, partial, edges)


def plan_for(mesh):
    return on_pair if mesh.shape["lon"] == 2 and mesh.shape["lev"] == 1 else on_device


def solution(mesh):
    return jax.shard_map(
        plan_for(mesh),
        mesh=mesh,
        in_specs=(
            P("member", "lev", "lat", "lon"),
            P("lev", "lat", "lon"),
            P(),
            P(),
            P(),
            P("lev"),
            P(),
            P(),
        ),
        out_specs=P("member", "lev", "lat", "lon"),
        check_vma=False,
    )
```

```python
import functools
import math

import jax
import jax.numpy as jnp
import ml_dtypes
import numpy as np
from jax import lax
from jax.experimental import pallas as pl
from jax.experimental.pallas import tpu as pltpu
from jax.sharding import PartitionSpec as P

KMAX = 1024
POLE_ROWS = 24


def extended(cells, sides, width, closed):
    for axis, dim in sides:
        count = lax.axis_size(axis)
        ends = count if closed else count - 1
        head = lax.slice_in_dim(cells, 0, width, axis=dim)
        tail = lax.slice_in_dim(cells, cells.shape[dim] - width, cells.shape[dim], axis=dim)
        cells = jnp.concatenate(
            [
                lax.ppermute(tail, axis, [(i, (i + 1) % count) for i in range(ends)]),
                cells,
                lax.ppermute(head, axis, [((i + 1) % count, i) for i in range(ends)]),
            ],
            axis=dim,
        )
    return cells


def entering(value, axis, join, neutral):
    count, mine = (lax.axis_size(axis), lax.axis_index(axis))
    pieces = lax.all_gather(value, axis)
    total = jnp.full_like(value, 0) + jnp.asarray(neutral, value.dtype)

    def turn(position, total):
        longer = join(total, pieces[position])
        return jnp.where(position < mine, longer, total)

    return lax.fori_loop(0, count - 1, turn, total)


def wave_table(col_count, wave_start, wave_count, circle):
    columns = lax.iota(jnp.int32, col_count)
    wave_index = wave_start + lax.iota(jnp.int32, wave_count)
    phase = columns[:, None] * wave_index[None, :] % circle
    angle = phase.astype(jnp.float32) * (2.0 * math.pi / circle)
    return jnp.concatenate([jnp.cos(angle), jnp.sin(angle)], axis=1)


def keep_weights(cut_rows, wave_start, wave_count, circle):
    wave_index = wave_start + lax.iota(jnp.int32, wave_count)
    factor = jnp.where(wave_index == 0, 1.0, 2.0) / circle
    kept = (wave_index[None, :] <= cut_rows[:, None]).astype(jnp.float32) * factor[None, :]
    return jnp.concatenate([kept, kept], axis=1)


def block_width():
    return min(KMAX, 128)


def project_rows(row_data, cut_rows):
    circle = row_data.shape[1]
    width = block_width()
    result = jnp.zeros(row_data.shape, jnp.float32)
    for block_index in range(KMAX // width):
        table = wave_table(circle, block_index * width, width, circle)
        coefs = jnp.dot(
            row_data, table, precision=lax.Precision.HIGHEST, preferred_element_type=jnp.float32
        )
        weights = keep_weights(cut_rows, block_index * width, width, circle)
        result = result + jnp.dot(
            coefs * weights,
            table.T,
            precision=lax.Precision.HIGHEST,
            preferred_element_type=jnp.float32,
        )
    return result


def transpose_filter(row_data, cut_rows, flag_rows):
    lon_count = lax.axis_size("lon")
    lon_index = lax.axis_index("lon")
    share = row_data.shape[0] // lon_count
    full_rows = lax.all_to_all(row_data, "lon", split_axis=0, concat_axis=1, tiled=True)
    my_cuts = lax.dynamic_slice_in_dim(cut_rows, lon_index * share, share)
    smoothed = project_rows(full_rows, my_cuts)
    returned = lax.all_to_all(smoothed, "lon", split_axis=1, concat_axis=0, tiled=True)
    return jnp.where(flag_rows[:, None] > 0, returned, row_data)


def polar_filter(row_data, cut_rows, flag_rows):
    return transpose_filter(row_data, cut_rows, flag_rows)


def on_device(adjoint, depth, zonal_coef, merid_coef, coriolis, layer_weight, cutoffs, polar_flags):
    fields, level_count, lat_rows, lon_cells = adjoint.shape
    lat_index = lax.axis_index("lat")
    lat_total = lat_rows * lax.axis_size("lat")
    stacked = adjoint.reshape(fields * level_count, lat_rows, lon_cells)
    bands = lax.all_to_all(stacked, "lat", split_axis=0, concat_axis=1, tiled=True)
    groups = bands.shape[0]
    polar_block = jnp.concatenate([bands[:, :POLE_ROWS], bands[:, lat_total - POLE_ROWS :]], axis=1)
    polar_cuts = jnp.concatenate([cutoffs[:POLE_ROWS], cutoffs[lat_total - POLE_ROWS :]])
    polar_marks = jnp.concatenate([polar_flags[:POLE_ROWS], polar_flags[lat_total - POLE_ROWS :]])
    row_data = polar_block.reshape(groups * 2 * POLE_ROWS, lon_cells)
    cut_rows = jnp.tile(polar_cuts, groups)
    flag_rows = jnp.tile(polar_marks, groups)
    treated = polar_filter(row_data, cut_rows, flag_rows)
    treated = treated.reshape(groups, 2 * POLE_ROWS, lon_cells)
    bands = jnp.concatenate(
        [
            treated[:, :POLE_ROWS],
            bands[:, POLE_ROWS : lat_total - POLE_ROWS],
            treated[:, POLE_ROWS:],
        ],
        axis=1,
    )
    filtered = lax.all_to_all(bands, "lat", split_axis=1, concat_axis=0, tiled=True).reshape(
        adjoint.shape
    )
    q_height = filtered[0]
    q_east = filtered[1]
    q_north = filtered[2]
    zonal_rows = lax.dynamic_slice_in_dim(zonal_coef, lat_index * lat_rows, lat_rows)[None, :, None]
    merid_rows = lax.dynamic_slice_in_dim(merid_coef, lat_index * lat_rows, lat_rows)[None, :, None]
    coriolis_rows = lax.dynamic_slice_in_dim(coriolis, lat_index * lat_rows, lat_rows)[
        None, :, None
    ]
    height_flux = depth.astype(jnp.float32) * q_height
    north_pair = jnp.stack([merid_rows * q_north, merid_rows * height_flux])
    north_rims = extended(north_pair, (("lat", 2),), 1, False)
    merid_diff = north_rims[:, :, :-2] - north_rims[:, :, 2:]
    east_pair = jnp.stack([q_east, height_flux])
    east_rims = extended(east_pair, (("lon", 3),), 1, True)
    zonal_diff = zonal_rows * (east_rims[..., :-2] - east_rims[..., 2:])
    column_force = -zonal_diff[0] - merid_diff[0]
    running = jnp.cumsum(column_force, axis=0)
    carried = entering(
        jnp.sum(column_force, axis=0), "lev", jnp.add, jnp.zeros((lat_rows, lon_cells), jnp.float32)
    )
    new_height = adjoint[0] + layer_weight[:, None, None] * (running + carried[None])
    new_east = adjoint[1] - zonal_diff[1] - coriolis_rows * q_north
    new_north = adjoint[2] - merid_diff[1] + coriolis_rows * q_east
    return jnp.stack([new_height, new_east, new_north])


REMOTE = 28
OWN = 28
OTHER = 30
FAR = 32
CODES = 80
PART = 8
GROUP = 2
TILE = 256
LANES = 128
ROWS = 8
ORDER = (2, 0, 1)
MESH = pl.DeviceIdType.MESH


def halves(value):
    high = value.astype(jnp.bfloat16)
    return high, (value - high.astype(jnp.float32)).astype(jnp.bfloat16)


def split_table(value):
    high = np.asarray(value, np.float32).astype(ml_dtypes.bfloat16)
    low = (np.asarray(value, np.float32) - high.astype(np.float32)).astype(ml_dtypes.bfloat16)
    return high, low


def factors(matrix, rank):
    u, s, v = np.linalg.svd(matrix, full_matrices=False)
    size = np.sqrt(s[:rank])
    return u[:, :rank] * size, v[:rank].T * size


@functools.lru_cache(maxsize=None)
def kernel_tables(cells):
    circle = 2 * cells

    def kernel(distance):
        wave = circle * np.sin(np.pi * (distance % (2 * circle)) / circle)
        return np.where(distance % circle == 0, 0.0, 1.0 / np.where(distance % circle == 0, 1.0, wave))

    n = np.arange(cells)
    here = kernel(n[:, None] - n[None, :])
    project = np.zeros((cells, LANES))
    expand = np.zeros((LANES, cells))
    left, right = factors(kernel(n[:, None] - n[None, :] - cells), REMOTE)
    project[:, :REMOTE] = right
    expand[:REMOTE] = left.T
    project[:, OWN] = kernel(cells - 1 - n)
    project[:, OWN + 1] = kernel(0 - n)
    project[:, OTHER] = kernel(cells - 1 - n - cells)
    project[:, OTHER + 1] = kernel(0 - n - cells)
    blocks = cells // TILE
    at = FAR
    for block in range(blocks):
        part = slice(block * TILE, (block + 1) * TILE)
        far = here[part].copy()
        far[:, part] = 0.0
        rank = 12 if block in (0, blocks - 1) else 18
        left, right = factors(far, rank)
        project[:, at : at + rank] = right
        expand[at : at + rank, part] = left.T
        at += rank
    split = cells // 2
    turned = np.roll(expand, 48, axis=0)
    groups = []
    for part in (expand[:CODES, :split], turned[:CODES, split:]):
        high, low = split_table(part)
        groups.append(np.concatenate([high, high, low, np.zeros((TILE - 3 * CODES, split), high.dtype)]))
    near = kernel(n[:TILE, None] - n[None, :TILE]).T
    project_high, project_low = split_table(project)
    near_high, near_low = split_table(near)
    return (
        np.concatenate([project_high, project_low], axis=1),
        np.concatenate(groups, axis=1),
        np.concatenate([near_high, near_high, near_low]),
    )


def column(ref, first, kind=jnp.float32):
    row = lax.broadcasted_iota(jnp.int32, (ROWS, LANES), 0)
    value = jnp.zeros((ROWS, LANES), kind)
    for turn in range(ROWS):
        value = jnp.where(row == turn, ref[first + turn], value)
    return value


def across(value, width):
    return jnp.concatenate([value] * (width // LANES), axis=1)


def filter_kernel(
    merid_hbm, cuts_hbm, flags_hbm, zonal_hbm, coriolis_hbm, weight_hbm, x_hbm, depth_hbm, project_hbm, expand_hbm, near_hbm,
    out_ref, edges_ref,
    merid_ref, cuts_ref, flags_ref, zonal_ref, coriolis_ref, weight_ref, q_ref, rims_ref, x_ref, depth_ref,
    project_ref, expand_ref, near_ref, high_ref, low_ref, code_ref, edge_ref, send_ref, take_ref,
    rows_ref, brink_ref, scalar_sem, load_sem, table_sem, out_sem, in_sem, leave_sem, reach_sem,
):
    fields, levels, rows, cells = x_ref.shape
    circle = 2 * cells
    count = levels * rows
    half = count // 2
    lat_count = lax.axis_size("lat")
    lat = lax.axis_index("lat")
    lon = lax.axis_index("lon")
    scalars = [
        pltpu.make_async_copy(source, target, scalar_sem.at[turn])
        for turn, (source, target) in enumerate(
            (
                (cuts_hbm, cuts_ref), (flags_hbm, flags_ref), (merid_hbm, merid_ref),
                (zonal_hbm, zonal_ref), (coriolis_hbm, coriolis_ref), (weight_hbm, weight_ref),
            )
        )
    ]
    for scalar in scalars:
        scalar.start()
    loads = {f: pltpu.make_async_copy(x_hbm.at[f], x_ref.at[f], load_sem.at[f]) for f in ORDER[1:]}
    quarters = [
        pltpu.make_async_copy(
            x_hbm.at[ORDER[0], pl.ds(start, 8)], x_ref.at[ORDER[0], pl.ds(start, 8)], load_sem.at[fields + start // 8]
        )
        for start in range(0, levels, 8)
    ]
    tables = [
        pltpu.make_async_copy(source, target, table_sem.at[turn])
        for turn, (source, target) in enumerate(
            ((project_hbm, project_ref), (depth_hbm, depth_ref), (near_hbm, near_ref), (expand_hbm, expand_ref))
        )
    ]
    for quarter in quarters:
        quarter.start()
    tables[0].start()
    loads[ORDER[1]].start()
    tables[1].start()
    loads[ORDER[2]].start()
    tables[2].start()
    tables[3].start()

    barrier = pltpu.get_barrier_semaphore()
    pl.semaphore_signal(barrier, inc=1, device_id={"lon": 1 - lon}, device_id_type=MESH)

    up = {"lat": jnp.minimum(lat + 1, lat_count - 1), "lon": jnp.where(lat < lat_count - 1, lon, 1 - lon)}
    down = {"lat": jnp.maximum(lat - 1, 0), "lon": jnp.where(lat > 0, lon, 1 - lon)}
    upward = [lat % 2, 1 - lat % 2]
    targets = [{name: jnp.where(way == 1, up[name], down[name]) for name in up} for way in upward]
    slots = [
        jnp.where(way == 1, jnp.where(lat < lat_count - 1, 0, 1), jnp.where(lat > 0, 1, 0)) for way in upward
    ]
    for target in targets:
        pl.semaphore_signal(barrier, inc=1, device_id=target, device_id_type=MESH)

    for scalar in scalars:
        scalar.wait()
    first = lat * rows
    cuts = column(cuts_ref, first, jnp.int32)
    on = jnp.where(column(flags_ref, first, jnp.int32) > 0, 1.0, 0.0)
    at_end = jnp.where(lat == 0, 0, jnp.where(lat == lat_count - 1, rows - 1, -1))
    row = lax.broadcasted_iota(jnp.int32, (rows, LANES), 0)
    merid = column(merid_ref, first)
    zonal = column(zonal_ref, first)
    coriolis = column(coriolis_ref, first)
    brink = jnp.where(row == at_end, 0.0, merid)
    kept = (2 * cuts + 1).astype(jnp.float32)
    keep = jnp.where(on > 0.0, kept * (1.0 / circle), 1.0)
    odd = jnp.bitwise_and(cuts, 1)
    sign = on * jnp.where(odd == 0, -1.0, 1.0)
    place = lax.broadcasted_iota(jnp.int32, (rows, cells), 1).astype(jnp.float32)
    phase = across(kept, cells) * place
    phase = phase - jnp.floor(phase * (1.0 / (2 * circle))) * (2.0 * circle)
    angle = phase * (math.pi / circle)
    cos = across(on, cells) * jnp.cos(angle)
    sin = across(on, cells) * jnp.sin(angle)
    lane = lax.broadcasted_iota(jnp.int32, (rows, LANES), 1)

    def at_edges(end, start, low):
        return jnp.where(lane == low, end, jnp.where(lane == low + 1, start, 0.0))

    end_cos, end_sin = cos[:, cells - 1 :], sin[:, cells - 1 :]
    start_cos, start_sin = cos[:, :1], sin[:, :1]
    mix_cos = at_edges(end_sin, start_sin, OWN) + at_edges(sign * end_cos, sign * start_cos, OTHER)
    mix_sin = at_edges(-end_cos, -start_cos, OWN) + at_edges(sign * end_sin, sign * start_sin, OTHER)
    rows_ref[0] = cos
    rows_ref[1] = sin

    def exchange(field):
        return pltpu.make_async_remote_copy(
            src_ref=send_ref.at[field], dst_ref=take_ref.at[field], send_sem=out_sem.at[field],
            recv_sem=in_sem.at[field], device_id={"lon": 1 - lon}, device_id_type=MESH,
        )

    def spread(value):
        return jnp.broadcast_to(value[None], (levels,) + value.shape).reshape(count, value.shape[1])

    groups = cells // TILE // GROUP

    def send(turn, which, group, slot):
        at = pl.ds(group * GROUP * TILE, GROUP * TILE)
        place = which * groups + group
        return pltpu.make_async_remote_copy(
            src_ref=brink_ref.at[upward[turn], which, :, at], dst_ref=edges_ref.at[slot, which, :, at],
            send_sem=leave_sem.at[turn, place], recv_sem=reach_sem.at[slot, place],
            device_id=targets[turn], device_id_type=MESH,
        )

    lane_all = lax.broadcasted_iota(jnp.int32, (count, LANES), 1)
    part = 8
    for turn, field in enumerate(ORDER):
        if field != ORDER[0]:
            loads[field].wait()
        for group in range(levels // part):
            if field == ORDER[0]:
                quarters[group].wait()
            x = x_ref[field, group * part : (group + 1) * part]
            for which in range(2):
                high, low = halves((x * rows_ref[which][None]).reshape(part * rows, cells))
                at = slice(which * count + group * part * rows, which * count + (group + 1) * part * rows)
                high_ref[field, at] = high
                low_ref[field, at] = low
        if turn == 0:
            tables[0].wait()
        table = project_ref[...]
        total = jnp.dot(high_ref[field], table, preferred_element_type=jnp.float32)
        total = total + jnp.dot(low_ref[field], table, preferred_element_type=jnp.float32)
        code = total[:, :LANES] + total[:, LANES:]
        code_ref[field] = code
        code_cos, code_sin = code[:count], code[count:]
        message = jnp.where(lane_all < 32, code_cos, pltpu.roll(code_sin, 32, 1))
        if field < 2:
            edge = spread(mix_cos) * code_cos + spread(mix_sin) * code_sin
            start, end = x_ref[field, :, :, :LANES], x_ref[field, :, :, cells - LANES :]
            start, end = start.reshape(count, LANES)[:, :1], end.reshape(count, LANES)[:, LANES - 1 :]
            edge = edge + spread(keep) * jnp.where(lane_all == OWN, end, jnp.where(lane_all == OWN + 1, start, 0.0))
            edge_ref[field] = edge
            message = jnp.where(jnp.logical_and(lane_all >= OWN, lane_all < OWN + 2), edge, message)
        if field == 0:
            tables[1].wait()
            start, end = depth_ref[:, :, :LANES], depth_ref[:, :, cells - LANES :]
            start = start.astype(jnp.float32).reshape(count, LANES)[:, :1]
            end = end.astype(jnp.float32).reshape(count, LANES)[:, LANES - 1 :]
            message = jnp.where(lane_all == OWN + 32, end, jnp.where(lane_all == OWN + 33, start, message))
        send_ref[field] = jnp.where(lane_all[:half] < 64, message[:half], pltpu.roll(message[half:], 64, 1))
        if turn == 0:
            pl.semaphore_wait(barrier, 3)
        exchange(field).start()

    tables[2].wait()
    tables[3].wait()
    lane_row = lax.broadcasted_iota(jnp.int32, (rows, LANES), 1)
    row_all = lax.broadcasted_iota(jnp.int32, (rows, cells), 0)

    def zonal_adjoint(value, rims):
        left, right = pltpu.roll(value, 1, 1), pltpu.roll(value, cells - 1, 1)
        left = jnp.concatenate([jnp.where(lane_row == 0, rims, left[:, :LANES]), left[:, LANES:]], axis=1)
        last = cells - LANES
        right = jnp.concatenate([right[:, :last], jnp.where(lane_row == LANES - 1, rims, right[:, last:])], axis=1)
        return across(zonal, cells) * (left - right)

    def merid_adjoint(value):
        value = across(merid, cells) * value
        up = jnp.where(row_all == 0, 0.0, pltpu.roll(value, 1, 0))
        down = jnp.where(row_all == rows - 1, 0.0, pltpu.roll(value, rows - 1, 0))
        return up - down

    def fluxes(level):
        north = q_ref[2, level]
        flux = depth_ref[level].astype(jnp.float32) * q_ref[0, level]
        out_ref[1, level] = x_ref[1, level] - zonal_adjoint(flux, rims_ref[0, level]) - across(coriolis, cells) * north
        out_ref[2, level] = x_ref[2, level] - merid_adjoint(flux)

    def forces(level, run):
        east = q_ref[1, level]
        run = run - (zonal_adjoint(east, rims_ref[1, level]) + merid_adjoint(q_ref[2, level]))
        out_ref[0, level] = x_ref[0, level] + weight_ref[level] * run
        out_ref[2, level] += across(coriolis, cells) * east
        return run

    for field in ORDER:
        exchange(field).wait_recv()
        taken = take_ref[field]
        taken = jnp.concatenate([taken, pltpu.roll(taken, 64, 1)])
        turned = pltpu.roll(taken, 96, 1)
        if field < 2:
            rims = taken + pltpu.roll(edge_ref[field], LANES - 2, 1)
            if field == 0:
                rims = rims * turned
            rims = jnp.where(
                lane_all == LANES - 1, pltpu.roll(rims, LANES - 2 - OWN, 1), pltpu.roll(rims, LANES - OWN, 1)
            )
            rims_ref[field] = rims.reshape(levels, rows, LANES)
        signs = spread(sign)
        code = code_ref[field]
        code = jnp.concatenate(
            [
                jnp.where(lane_all < REMOTE, signs * turned, code[:count]),
                jnp.where(lane_all < REMOTE, -signs * taken, code[count:]),
            ]
        )
        code_high = code.astype(jnp.bfloat16).astype(jnp.float32)
        code_low = code - code_high
        lane_both = lax.broadcasted_iota(jnp.int32, code.shape, 1)
        packed = []
        for low, head, rest in (
            (pltpu.roll(code_low, CODES, 1), code_high, pltpu.roll(code_high, 32, 1)),
            (code_low, pltpu.roll(code_high, 48, 1), pltpu.roll(code_high, 80, 1)),
        ):
            pair = (jnp.where(lane_both < CODES, head, low), jnp.where(lane_both < 32, low, rest))
            packed.append([value.astype(jnp.bfloat16) for value in pair])
        for block in range(cells // TILE):
            at = slice(block * TILE, (block + 1) * TILE)
            high, low = high_ref[field, :, at], low_ref[field, :, at]
            terms = jnp.concatenate([high, low, high, *packed[2 * at.start // cells]], axis=1)
            weights = jnp.concatenate([near_ref[...], expand_ref[:, at]], axis=0)
            value = jnp.dot(terms, weights, preferred_element_type=jnp.float32)
            shape = (levels, rows, TILE)
            result = across(keep, TILE)[None] * x_ref[field, :, :, at]
            result = result + rows_ref[1, :, at][None] * value[:count].reshape(shape)
            result = result - rows_ref[0, :, at][None] * value[count:].reshape(shape)
            q_ref[field, :, :, at] = result
            turns = range(block * levels * TILE // cells, (block + 1) * levels * TILE // cells)
            for level in turns if field == 1 else ():
                fluxes(level)
            if field != 1:
                edge = result
                if field == 0:
                    edge = result * depth_ref[:, :, at].astype(jnp.float32)
                edge = edge * across(brink, TILE)[None]
                which = 0 if field == 2 else 1
                brink_ref[0, which, :, at] = edge[:, 0, :]
                brink_ref[1, which, :, at] = edge[:, rows - 1, :]
                if block % GROUP == GROUP - 1:
                    for turn in range(2):
                        send(turn, which, block // GROUP, slots[turn]).start()

    def tail(step, run):
        for turn in range(8):
            level = step * 8 + turn
            run = forces(level, run)
        return run

    lax.fori_loop(0, levels // 8, tail, jnp.zeros((rows, cells), jnp.float32))
    for field in ORDER:
        exchange(field).wait_send()

    for which in range(2):
        for group in range(groups):
            for turn in range(2):
                send(turn, which, group, slots[turn]).wait_send()
                send(turn, which, group, turn).wait_recv()


def final_kernel(weight_ref, part_ref, edges_ref, out_hbm, done_ref, sems):
    _, levels, rows, cells = part_ref.shape
    row = lax.broadcasted_iota(jnp.int32, (rows, cells), 0)
    copies = [pltpu.make_async_copy(part_ref.at[1], out_hbm.at[1], sems.at[0])]
    copies[0].start()

    def missing(which, level):
        before, after = edges_ref[0, which, level : level + 1, :], edges_ref[1, which, level : level + 1, :]
        return jnp.where(row == 0, before, jnp.where(row == rows - 1, -after, 0.0))

    run = jnp.zeros((rows, cells), jnp.float32)
    for level in range(levels):
        run = run - missing(0, level)
        done_ref[0, level] = part_ref[0, level] + weight_ref[level] * run
        done_ref[1, level] = part_ref[2, level] - missing(1, level)
        if level % PART == PART - 1:
            at = pl.ds(level - PART + 1, PART)
            for turn, field in enumerate((0, 2)):
                copies.append(
                    pltpu.make_async_copy(done_ref.at[turn, at], out_hbm.at[field, at], sems.at[len(copies)])
                )
                copies[-1].start()
    for copy in copies:
        copy.wait()


def on_pair(adjoint, depth, zonal_coef, merid_coef, coriolis, layer_weight, cutoffs, polar_flags):
    fields, level_count, rows, cells = adjoint.shape
    project, expand, near = (jnp.asarray(table) for table in kernel_tables(cells))
    count = level_count * rows
    pieces = cells // TILE // GROUP
    scalars = pl.BlockSpec(memory_space=pltpu.SMEM)
    there = pl.BlockSpec(memory_space=pltpu.HBM)
    close = pl.BlockSpec(memory_space=pltpu.VMEM)
    single = jnp.float32
    dma = pltpu.SemaphoreType.DMA

    partial, edges = pl.pallas_call(
        filter_kernel,
        in_specs=[there] * 11,
        out_specs=[close] * 2,
        out_shape=[
            jax.ShapeDtypeStruct(adjoint.shape, single),
            jax.ShapeDtypeStruct((2, 2, level_count, cells), single),
        ],
        scratch_shapes=[
            pltpu.SMEM(merid_coef.shape, single),
            pltpu.SMEM(cutoffs.shape, jnp.int32),
            pltpu.SMEM(polar_flags.shape, jnp.int32),
            pltpu.SMEM(zonal_coef.shape, single),
            pltpu.SMEM(coriolis.shape, single),
            pltpu.SMEM(layer_weight.shape, single),
            pltpu.VMEM(adjoint.shape, single),
            pltpu.VMEM((2, level_count, rows, LANES), single),
            pltpu.VMEM(adjoint.shape, single),
            pltpu.VMEM(depth.shape, depth.dtype),
            pltpu.VMEM(project.shape, project.dtype),
            pltpu.VMEM(expand.shape, expand.dtype),
            pltpu.VMEM(near.shape, near.dtype),
            pltpu.VMEM((fields, 2 * count, cells), jnp.bfloat16),
            pltpu.VMEM((fields, 2 * count, cells), jnp.bfloat16),
            pltpu.VMEM((fields, 2 * count, LANES), single),
            pltpu.VMEM((2, count, LANES), single),
            pltpu.VMEM((fields, count // 2, LANES), single),
            pltpu.VMEM((fields, count // 2, LANES), single),
            pltpu.VMEM((2, rows, cells), single),
            pltpu.VMEM((2, 2, level_count, cells), single),
            dma((6,)),
            dma((3 + level_count // 8,)),
            dma((4,)),
            dma((3,)),
            dma((3,)),
            dma((2, 2 * pieces)),
            dma((2, 2 * pieces)),
        ],
        compiler_params=pltpu.CompilerParams(
            collective_id=0, has_side_effects=True, vmem_limit_bytes=36 * 2**20
        ),
    )(*(pltpu.with_memory_space_constraint(value, pltpu.HBM) for value in (merid_coef, cutoffs, polar_flags, zonal_coef, coriolis, layer_weight, adjoint, depth, project, expand, near)))

    return pl.pallas_call(
        final_kernel,
        in_specs=[scalars] + [close] * 2,
        out_specs=pl.BlockSpec(memory_space=pl.ANY),
        out_shape=jax.ShapeDtypeStruct(adjoint.shape, single),
        scratch_shapes=[pltpu.VMEM((2,) + adjoint.shape[1:], single), dma((1 + 2 * level_count // PART,))],
        compiler_params=pltpu.CompilerParams(vmem_limit_bytes=32 * 2**20),
    )(layer_weight, partial, edges)


def plan_for(mesh):
    return on_pair if mesh.shape["lon"] == 2 and mesh.shape["lev"] == 1 else on_device


def solution(mesh):
    return jax.shard_map(
        plan_for(mesh),
        mesh=mesh,
        in_specs=(
            P("member", "lev", "lat", "lon"),
            P("lev", "lat", "lon"),
            P(),
            P(),
            P(),
            P("lev"),
            P(),
            P(),
        ),
        out_specs=P("member", "lev", "lat", "lon"),
        check_vma=False,
    )
```

```python
import functools
import math

import jax
import jax.numpy as jnp
import ml_dtypes
import numpy as np
from jax import lax
from jax.experimental import pallas as pl
from jax.experimental.pallas import tpu as pltpu
from jax.sharding import PartitionSpec as P

KMAX = 1024
POLE_ROWS = 24


def extended(cells, sides, width, closed):
    for axis, dim in sides:
        count = lax.axis_size(axis)
        ends = count if closed else count - 1
        head = lax.slice_in_dim(cells, 0, width, axis=dim)
        tail = lax.slice_in_dim(cells, cells.shape[dim] - width, cells.shape[dim], axis=dim)
        cells = jnp.concatenate(
            [
                lax.ppermute(tail, axis, [(i, (i + 1) % count) for i in range(ends)]),
                cells,
                lax.ppermute(head, axis, [((i + 1) % count, i) for i in range(ends)]),
            ],
            axis=dim,
        )
    return cells


def entering(value, axis, join, neutral):
    count, mine = (lax.axis_size(axis), lax.axis_index(axis))
    pieces = lax.all_gather(value, axis)
    total = jnp.full_like(value, 0) + jnp.asarray(neutral, value.dtype)

    def turn(position, total):
        longer = join(total, pieces[position])
        return jnp.where(position < mine, longer, total)

    return lax.fori_loop(0, count - 1, turn, total)


def wave_table(col_count, wave_start, wave_count, circle):
    columns = lax.iota(jnp.int32, col_count)
    wave_index = wave_start + lax.iota(jnp.int32, wave_count)
    phase = columns[:, None] * wave_index[None, :] % circle
    angle = phase.astype(jnp.float32) * (2.0 * math.pi / circle)
    return jnp.concatenate([jnp.cos(angle), jnp.sin(angle)], axis=1)


def keep_weights(cut_rows, wave_start, wave_count, circle):
    wave_index = wave_start + lax.iota(jnp.int32, wave_count)
    factor = jnp.where(wave_index == 0, 1.0, 2.0) / circle
    kept = (wave_index[None, :] <= cut_rows[:, None]).astype(jnp.float32) * factor[None, :]
    return jnp.concatenate([kept, kept], axis=1)


def block_width():
    return min(KMAX, 128)


def project_rows(row_data, cut_rows):
    circle = row_data.shape[1]
    width = block_width()
    result = jnp.zeros(row_data.shape, jnp.float32)
    for block_index in range(KMAX // width):
        table = wave_table(circle, block_index * width, width, circle)
        coefs = jnp.dot(
            row_data, table, precision=lax.Precision.HIGHEST, preferred_element_type=jnp.float32
        )
        weights = keep_weights(cut_rows, block_index * width, width, circle)
        result = result + jnp.dot(
            coefs * weights,
            table.T,
            precision=lax.Precision.HIGHEST,
            preferred_element_type=jnp.float32,
        )
    return result


def transpose_filter(row_data, cut_rows, flag_rows):
    lon_count = lax.axis_size("lon")
    lon_index = lax.axis_index("lon")
    share = row_data.shape[0] // lon_count
    full_rows = lax.all_to_all(row_data, "lon", split_axis=0, concat_axis=1, tiled=True)
    my_cuts = lax.dynamic_slice_in_dim(cut_rows, lon_index * share, share)
    smoothed = project_rows(full_rows, my_cuts)
    returned = lax.all_to_all(smoothed, "lon", split_axis=1, concat_axis=0, tiled=True)
    return jnp.where(flag_rows[:, None] > 0, returned, row_data)


def polar_filter(row_data, cut_rows, flag_rows):
    return transpose_filter(row_data, cut_rows, flag_rows)


def on_device(adjoint, depth, zonal_coef, merid_coef, coriolis, layer_weight, cutoffs, polar_flags):
    fields, level_count, lat_rows, lon_cells = adjoint.shape
    lat_index = lax.axis_index("lat")
    lat_total = lat_rows * lax.axis_size("lat")
    stacked = adjoint.reshape(fields * level_count, lat_rows, lon_cells)
    bands = lax.all_to_all(stacked, "lat", split_axis=0, concat_axis=1, tiled=True)
    groups = bands.shape[0]
    polar_block = jnp.concatenate([bands[:, :POLE_ROWS], bands[:, lat_total - POLE_ROWS :]], axis=1)
    polar_cuts = jnp.concatenate([cutoffs[:POLE_ROWS], cutoffs[lat_total - POLE_ROWS :]])
    polar_marks = jnp.concatenate([polar_flags[:POLE_ROWS], polar_flags[lat_total - POLE_ROWS :]])
    row_data = polar_block.reshape(groups * 2 * POLE_ROWS, lon_cells)
    cut_rows = jnp.tile(polar_cuts, groups)
    flag_rows = jnp.tile(polar_marks, groups)
    treated = polar_filter(row_data, cut_rows, flag_rows)
    treated = treated.reshape(groups, 2 * POLE_ROWS, lon_cells)
    bands = jnp.concatenate(
        [
            treated[:, :POLE_ROWS],
            bands[:, POLE_ROWS : lat_total - POLE_ROWS],
            treated[:, POLE_ROWS:],
        ],
        axis=1,
    )
    filtered = lax.all_to_all(bands, "lat", split_axis=1, concat_axis=0, tiled=True).reshape(
        adjoint.shape
    )
    q_height = filtered[0]
    q_east = filtered[1]
    q_north = filtered[2]
    zonal_rows = lax.dynamic_slice_in_dim(zonal_coef, lat_index * lat_rows, lat_rows)[None, :, None]
    merid_rows = lax.dynamic_slice_in_dim(merid_coef, lat_index * lat_rows, lat_rows)[None, :, None]
    coriolis_rows = lax.dynamic_slice_in_dim(coriolis, lat_index * lat_rows, lat_rows)[
        None, :, None
    ]
    height_flux = depth.astype(jnp.float32) * q_height
    north_pair = jnp.stack([merid_rows * q_north, merid_rows * height_flux])
    north_rims = extended(north_pair, (("lat", 2),), 1, False)
    merid_diff = north_rims[:, :, :-2] - north_rims[:, :, 2:]
    east_pair = jnp.stack([q_east, height_flux])
    east_rims = extended(east_pair, (("lon", 3),), 1, True)
    zonal_diff = zonal_rows * (east_rims[..., :-2] - east_rims[..., 2:])
    column_force = -zonal_diff[0] - merid_diff[0]
    running = jnp.cumsum(column_force, axis=0)
    carried = entering(
        jnp.sum(column_force, axis=0), "lev", jnp.add, jnp.zeros((lat_rows, lon_cells), jnp.float32)
    )
    new_height = adjoint[0] + layer_weight[:, None, None] * (running + carried[None])
    new_east = adjoint[1] - zonal_diff[1] - coriolis_rows * q_north
    new_north = adjoint[2] - merid_diff[1] + coriolis_rows * q_east
    return jnp.stack([new_height, new_east, new_north])


REMOTE = 28
OWN = 28
OTHER = 30
FAR = 32
CODES = 80
PART = 8
GROUP = 2
TILE = 256
LANES = 128
ROWS = 8
ORDER = (2, 0, 1)
MESH = pl.DeviceIdType.MESH


def halves(value):
    high = value.astype(jnp.bfloat16)
    return high, (value - high.astype(jnp.float32)).astype(jnp.bfloat16)


def split_table(value):
    high = np.asarray(value, np.float32).astype(ml_dtypes.bfloat16)
    low = (np.asarray(value, np.float32) - high.astype(np.float32)).astype(ml_dtypes.bfloat16)
    return high, low


def factors(matrix, rank):
    u, s, v = np.linalg.svd(matrix, full_matrices=False)
    size = np.sqrt(s[:rank])
    return u[:, :rank] * size, v[:rank].T * size


@functools.lru_cache(maxsize=None)
def kernel_tables(cells):
    circle = 2 * cells

    def kernel(distance):
        wave = circle * np.sin(np.pi * (distance % (2 * circle)) / circle)
        return np.where(distance % circle == 0, 0.0, 1.0 / np.where(distance % circle == 0, 1.0, wave))

    n = np.arange(cells)
    here = kernel(n[:, None] - n[None, :])
    project = np.zeros((cells, LANES))
    expand = np.zeros((LANES, cells))
    left, right = factors(kernel(n[:, None] - n[None, :] - cells), REMOTE)
    project[:, :REMOTE] = right
    expand[:REMOTE] = left.T
    project[:, OWN] = kernel(cells - 1 - n)
    project[:, OWN + 1] = kernel(0 - n)
    project[:, OTHER] = kernel(cells - 1 - n - cells)
    project[:, OTHER + 1] = kernel(0 - n - cells)
    blocks = cells // TILE
    at = FAR
    for block in range(blocks):
        part = slice(block * TILE, (block + 1) * TILE)
        far = here[part].copy()
        far[:, part] = 0.0
        rank = 12 if block in (0, blocks - 1) else 18
        left, right = factors(far, rank)
        project[:, at : at + rank] = right
        expand[at : at + rank, part] = left.T
        at += rank
    split = cells // 2
    turned = np.roll(expand, 48, axis=0)
    groups = []
    for part in (expand[:CODES, :split], turned[:CODES, split:]):
        high, low = split_table(part)
        groups.append(np.concatenate([high, high, low, np.zeros((TILE - 3 * CODES, split), high.dtype)]))
    near = kernel(n[:TILE, None] - n[None, :TILE]).T
    project_high, project_low = split_table(project)
    near_high, near_low = split_table(near)
    return (
        np.concatenate([project_high, project_low], axis=1),
        np.concatenate(groups, axis=1),
        np.concatenate([near_high, near_high, near_low]),
    )


def column(ref, first, kind=jnp.float32):
    row = lax.broadcasted_iota(jnp.int32, (ROWS, LANES), 0)
    value = jnp.zeros((ROWS, LANES), kind)
    for turn in range(ROWS):
        value = jnp.where(row == turn, ref[first + turn], value)
    return value


def across(value, width):
    return jnp.concatenate([value] * (width // LANES), axis=1)


def filter_kernel(
    merid_hbm, cuts_hbm, flags_hbm, zonal_hbm, coriolis_hbm, weight_hbm, x_hbm, depth_hbm, project_hbm, expand_hbm, near_hbm,
    out_ref, edges_ref,
    merid_ref, cuts_ref, flags_ref, zonal_ref, coriolis_ref, weight_ref, q_ref, rims_ref, x_ref, depth_ref,
    project_ref, expand_ref, near_ref, high_ref, low_ref, code_ref, edge_ref, send_ref, take_ref,
    rows_ref, brink_ref, scalar_sem, load_sem, table_sem, out_sem, in_sem, leave_sem, reach_sem,
):
    fields, levels, rows, cells = x_ref.shape
    circle = 2 * cells
    count = levels * rows
    half = count // 2
    lat_count = lax.axis_size("lat")
    lat = lax.axis_index("lat")
    lon = lax.axis_index("lon")
    scalars = [
        pltpu.make_async_copy(source, target, scalar_sem.at[turn])
        for turn, (source, target) in enumerate(
            (
                (cuts_hbm, cuts_ref), (flags_hbm, flags_ref), (merid_hbm, merid_ref),
                (zonal_hbm, zonal_ref), (coriolis_hbm, coriolis_ref), (weight_hbm, weight_ref),
            )
        )
    ]
    for scalar in scalars:
        scalar.start()
    loads = {f: pltpu.make_async_copy(x_hbm.at[f], x_ref.at[f], load_sem.at[f]) for f in ORDER[1:]}
    quarters = [
        pltpu.make_async_copy(
            x_hbm.at[ORDER[0], pl.ds(start, 8)], x_ref.at[ORDER[0], pl.ds(start, 8)], load_sem.at[fields + start // 8]
        )
        for start in range(0, levels, 8)
    ]
    tables = [
        pltpu.make_async_copy(source, target, table_sem.at[turn])
        for turn, (source, target) in enumerate(
            ((project_hbm, project_ref), (depth_hbm, depth_ref), (near_hbm, near_ref), (expand_hbm, expand_ref))
        )
    ]
    for quarter in quarters:
        quarter.start()
    tables[0].start()
    loads[ORDER[1]].start()
    tables[1].start()
    loads[ORDER[2]].start()
    tables[2].start()
    tables[3].start()

    barrier = pltpu.get_barrier_semaphore()
    pl.semaphore_signal(barrier, inc=1, device_id={"lon": 1 - lon}, device_id_type=MESH)

    up = {"lat": jnp.minimum(lat + 1, lat_count - 1), "lon": jnp.where(lat < lat_count - 1, lon, 1 - lon)}
    down = {"lat": jnp.maximum(lat - 1, 0), "lon": jnp.where(lat > 0, lon, 1 - lon)}
    upward = [lat % 2, 1 - lat % 2]
    targets = [{name: jnp.where(way == 1, up[name], down[name]) for name in up} for way in upward]
    slots = [
        jnp.where(way == 1, jnp.where(lat < lat_count - 1, 0, 1), jnp.where(lat > 0, 1, 0)) for way in upward
    ]
    for target in targets:
        pl.semaphore_signal(barrier, inc=1, device_id=target, device_id_type=MESH)

    for scalar in scalars:
        scalar.wait()
    first = lat * rows
    cuts = column(cuts_ref, first, jnp.int32)
    on = jnp.where(column(flags_ref, first, jnp.int32) > 0, 1.0, 0.0)
    at_end = jnp.where(lat == 0, 0, jnp.where(lat == lat_count - 1, rows - 1, -1))
    row = lax.broadcasted_iota(jnp.int32, (rows, LANES), 0)
    merid = column(merid_ref, first)
    zonal = column(zonal_ref, first)
    coriolis = column(coriolis_ref, first)
    brink = jnp.where(row == at_end, 0.0, merid)
    kept = (2 * cuts + 1).astype(jnp.float32)
    keep = jnp.where(on > 0.0, kept * (1.0 / circle), 1.0)
    odd = jnp.bitwise_and(cuts, 1)
    sign = on * jnp.where(odd == 0, -1.0, 1.0)
    place = lax.broadcasted_iota(jnp.int32, (rows, cells), 1).astype(jnp.float32)
    phase = across(kept, cells) * place
    phase = phase - jnp.floor(phase * (1.0 / (2 * circle))) * (2.0 * circle)
    angle = phase * (math.pi / circle)
    cos = across(on, cells) * jnp.cos(angle)
    sin = across(on, cells) * jnp.sin(angle)
    lane = lax.broadcasted_iota(jnp.int32, (rows, LANES), 1)

    def at_edges(end, start, low):
        return jnp.where(lane == low, end, jnp.where(lane == low + 1, start, 0.0))

    end_cos, end_sin = cos[:, cells - 1 :], sin[:, cells - 1 :]
    start_cos, start_sin = cos[:, :1], sin[:, :1]
    mix_cos = at_edges(end_sin, start_sin, OWN) + at_edges(sign * end_cos, sign * start_cos, OTHER)
    mix_sin = at_edges(-end_cos, -start_cos, OWN) + at_edges(sign * end_sin, sign * start_sin, OTHER)
    rows_ref[0] = cos
    rows_ref[1] = sin

    def exchange(field):
        return pltpu.make_async_remote_copy(
            src_ref=send_ref.at[field], dst_ref=take_ref.at[field], send_sem=out_sem.at[field],
            recv_sem=in_sem.at[field], device_id={"lon": 1 - lon}, device_id_type=MESH,
        )

    def spread(value):
        return jnp.broadcast_to(value[None], (levels,) + value.shape).reshape(count, value.shape[1])

    groups = cells // TILE // GROUP

    def send(turn, which, group, slot):
        at = pl.ds(group * GROUP * TILE, GROUP * TILE)
        place = which * groups + group
        return pltpu.make_async_remote_copy(
            src_ref=brink_ref.at[upward[turn], which, :, at], dst_ref=edges_ref.at[slot, which, :, at],
            send_sem=leave_sem.at[turn, place], recv_sem=reach_sem.at[slot, place],
            device_id=targets[turn], device_id_type=MESH,
        )

    lane_all = lax.broadcasted_iota(jnp.int32, (count, LANES), 1)
    part = 8
    for turn, field in enumerate(ORDER):
        if field != ORDER[0]:
            loads[field].wait()
        for group in range(levels // part):
            if field == ORDER[0]:
                quarters[group].wait()
            x = x_ref[field, group * part : (group + 1) * part]
            for which in range(2):
                high, low = halves((x * rows_ref[which][None]).reshape(part * rows, cells))
                at = slice(which * count + group * part * rows, which * count + (group + 1) * part * rows)
                high_ref[field, at] = high
                low_ref[field, at] = low
        if turn == 0:
            tables[0].wait()
        table = project_ref[...]
        total = jnp.dot(high_ref[field], table, preferred_element_type=jnp.float32)
        total = total + jnp.dot(low_ref[field], table, preferred_element_type=jnp.float32)
        code = total[:, :LANES] + total[:, LANES:]
        code_ref[field] = code
        code_cos, code_sin = code[:count], code[count:]
        message = jnp.where(lane_all < 32, code_cos, pltpu.roll(code_sin, 32, 1))
        if field < 2:
            edge = spread(mix_cos) * code_cos + spread(mix_sin) * code_sin
            start, end = x_ref[field, :, :, :LANES], x_ref[field, :, :, cells - LANES :]
            start, end = start.reshape(count, LANES)[:, :1], end.reshape(count, LANES)[:, LANES - 1 :]
            edge = edge + spread(keep) * jnp.where(lane_all == OWN, end, jnp.where(lane_all == OWN + 1, start, 0.0))
            edge_ref[field] = edge
            message = jnp.where(jnp.logical_and(lane_all >= OWN, lane_all < OWN + 2), edge, message)
        if field == 0:
            tables[1].wait()
            start, end = depth_ref[:, :, :LANES], depth_ref[:, :, cells - LANES :]
            start = start.astype(jnp.float32).reshape(count, LANES)[:, :1]
            end = end.astype(jnp.float32).reshape(count, LANES)[:, LANES - 1 :]
            message = jnp.where(lane_all == OWN + 32, end, jnp.where(lane_all == OWN + 33, start, message))
        send_ref[field] = jnp.where(lane_all[:half] < 64, message[:half], pltpu.roll(message[half:], 64, 1))
        if turn == 0:
            pl.semaphore_wait(barrier, 3)
        exchange(field).start()

    tables[2].wait()
    tables[3].wait()
    lane_row = lax.broadcasted_iota(jnp.int32, (rows, LANES), 1)
    row_all = lax.broadcasted_iota(jnp.int32, (rows, cells), 0)

    def zonal_adjoint(value, rims):
        left, right = pltpu.roll(value, 1, 1), pltpu.roll(value, cells - 1, 1)
        left = jnp.concatenate([jnp.where(lane_row == 0, rims, left[:, :LANES]), left[:, LANES:]], axis=1)
        last = cells - LANES
        right = jnp.concatenate([right[:, :last], jnp.where(lane_row == LANES - 1, rims, right[:, last:])], axis=1)
        return across(zonal, cells) * (left - right)

    def merid_adjoint(value):
        value = across(merid, cells) * value
        up = jnp.where(row_all == 0, 0.0, pltpu.roll(value, 1, 0))
        down = jnp.where(row_all == rows - 1, 0.0, pltpu.roll(value, rows - 1, 0))
        return up - down

    def fluxes(level):
        north = q_ref[2, level]
        flux = depth_ref[level].astype(jnp.float32) * q_ref[0, level]
        out_ref[1, level] = x_ref[1, level] - zonal_adjoint(flux, rims_ref[0, level]) - across(coriolis, cells) * north
        out_ref[2, level] = x_ref[2, level] - merid_adjoint(flux)

    def forces(level, run):
        east = q_ref[1, level]
        run = run - (zonal_adjoint(east, rims_ref[1, level]) + merid_adjoint(q_ref[2, level]))
        out_ref[0, level] = x_ref[0, level] + weight_ref[level] * run
        out_ref[2, level] += across(coriolis, cells) * east
        return run

    for field in ORDER:
        exchange(field).wait_recv()
        taken = take_ref[field]
        taken = jnp.concatenate([taken, pltpu.roll(taken, 64, 1)])
        turned = pltpu.roll(taken, 96, 1)
        if field < 2:
            rims = taken + pltpu.roll(edge_ref[field], LANES - 2, 1)
            if field == 0:
                rims = rims * turned
            rims = jnp.where(
                lane_all == LANES - 1, pltpu.roll(rims, LANES - 2 - OWN, 1), pltpu.roll(rims, LANES - OWN, 1)
            )
            rims_ref[field] = rims.reshape(levels, rows, LANES)
        signs = spread(sign)
        code = code_ref[field]
        code = jnp.concatenate(
            [
                jnp.where(lane_all < REMOTE, signs * turned, code[:count]),
                jnp.where(lane_all < REMOTE, -signs * taken, code[count:]),
            ]
        )
        code_high = code.astype(jnp.bfloat16).astype(jnp.float32)
        code_low = code - code_high
        lane_both = lax.broadcasted_iota(jnp.int32, code.shape, 1)
        packed = []
        for low, head, rest in (
            (pltpu.roll(code_low, CODES, 1), code_high, pltpu.roll(code_high, 32, 1)),
            (code_low, pltpu.roll(code_high, 48, 1), pltpu.roll(code_high, 80, 1)),
        ):
            pair = (jnp.where(lane_both < CODES, head, low), jnp.where(lane_both < 32, low, rest))
            packed.append([value.astype(jnp.bfloat16) for value in pair])
        for block in range(cells // TILE):
            at = slice(block * TILE, (block + 1) * TILE)
            high, low = high_ref[field, :, at], low_ref[field, :, at]
            terms = jnp.concatenate([high, low, high, *packed[2 * at.start // cells]], axis=1)
            weights = jnp.concatenate([near_ref[...], expand_ref[:, at]], axis=0)
            value = jnp.dot(terms, weights, preferred_element_type=jnp.float32)
            shape = (levels, rows, TILE)
            result = across(keep, TILE)[None] * x_ref[field, :, :, at]
            result = result + rows_ref[1, :, at][None] * value[:count].reshape(shape)
            result = result - rows_ref[0, :, at][None] * value[count:].reshape(shape)
            q_ref[field, :, :, at] = result
            turns = range(block * levels * TILE // cells, (block + 1) * levels * TILE // cells)
            for level in turns if field == 1 else ():
                fluxes(level)
            if field != 1:
                edge = result
                if field == 0:
                    edge = result * depth_ref[:, :, at].astype(jnp.float32)
                edge = edge * across(brink, TILE)[None]
                which = 0 if field == 2 else 1
                brink_ref[0, which, :, at] = edge[:, 0, :]
                brink_ref[1, which, :, at] = edge[:, rows - 1, :]
                if block % GROUP == GROUP - 1:
                    for turn in range(2):
                        send(turn, which, block // GROUP, slots[turn]).start()

    def tail(step, run):
        for turn in range(16):
            level = step * 16 + turn
            run = forces(level, run)
        return run

    lax.fori_loop(0, levels // 16, tail, jnp.zeros((rows, cells), jnp.float32))
    for field in ORDER:
        exchange(field).wait_send()

    for which in range(2):
        for group in range(groups):
            for turn in range(2):
                send(turn, which, group, slots[turn]).wait_send()
                send(turn, which, group, turn).wait_recv()


def final_kernel(weight_ref, part_ref, edges_ref, out_hbm, done_ref, sems):
    _, levels, rows, cells = part_ref.shape
    row = lax.broadcasted_iota(jnp.int32, (rows, cells), 0)
    copies = [pltpu.make_async_copy(part_ref.at[1], out_hbm.at[1], sems.at[0])]
    copies[0].start()

    def missing(which, level):
        before, after = edges_ref[0, which, level : level + 1, :], edges_ref[1, which, level : level + 1, :]
        return jnp.where(row == 0, before, jnp.where(row == rows - 1, -after, 0.0))

    run = jnp.zeros((rows, cells), jnp.float32)
    for level in range(levels):
        run = run - missing(0, level)
        done_ref[0, level] = part_ref[0, level] + weight_ref[level] * run
        done_ref[1, level] = part_ref[2, level] - missing(1, level)
        if level % PART == PART - 1:
            at = pl.ds(level - PART + 1, PART)
            for turn, field in enumerate((0, 2)):
                copies.append(
                    pltpu.make_async_copy(done_ref.at[turn, at], out_hbm.at[field, at], sems.at[len(copies)])
                )
                copies[-1].start()
    for copy in copies:
        copy.wait()


def on_pair(adjoint, depth, zonal_coef, merid_coef, coriolis, layer_weight, cutoffs, polar_flags):
    fields, level_count, rows, cells = adjoint.shape
    project, expand, near = (jnp.asarray(table) for table in kernel_tables(cells))
    count = level_count * rows
    pieces = cells // TILE // GROUP
    scalars = pl.BlockSpec(memory_space=pltpu.SMEM)
    there = pl.BlockSpec(memory_space=pltpu.HBM)
    close = pl.BlockSpec(memory_space=pltpu.VMEM)
    single = jnp.float32
    dma = pltpu.SemaphoreType.DMA

    partial, edges = pl.pallas_call(
        filter_kernel,
        in_specs=[there] * 11,
        out_specs=[close] * 2,
        out_shape=[
            jax.ShapeDtypeStruct(adjoint.shape, single),
            jax.ShapeDtypeStruct((2, 2, level_count, cells), single),
        ],
        scratch_shapes=[
            pltpu.SMEM(merid_coef.shape, single),
            pltpu.SMEM(cutoffs.shape, jnp.int32),
            pltpu.SMEM(polar_flags.shape, jnp.int32),
            pltpu.SMEM(zonal_coef.shape, single),
            pltpu.SMEM(coriolis.shape, single),
            pltpu.SMEM(layer_weight.shape, single),
            pltpu.VMEM(adjoint.shape, single),
            pltpu.VMEM((2, level_count, rows, LANES), single),
            pltpu.VMEM(adjoint.shape, single),
            pltpu.VMEM(depth.shape, depth.dtype),
            pltpu.VMEM(project.shape, project.dtype),
            pltpu.VMEM(expand.shape, expand.dtype),
            pltpu.VMEM(near.shape, near.dtype),
            pltpu.VMEM((fields, 2 * count, cells), jnp.bfloat16),
            pltpu.VMEM((fields, 2 * count, cells), jnp.bfloat16),
            pltpu.VMEM((fields, 2 * count, LANES), single),
            pltpu.VMEM((2, count, LANES), single),
            pltpu.VMEM((fields, count // 2, LANES), single),
            pltpu.VMEM((fields, count // 2, LANES), single),
            pltpu.VMEM((2, rows, cells), single),
            pltpu.VMEM((2, 2, level_count, cells), single),
            dma((6,)),
            dma((3 + level_count // 8,)),
            dma((4,)),
            dma((3,)),
            dma((3,)),
            dma((2, 2 * pieces)),
            dma((2, 2 * pieces)),
        ],
        compiler_params=pltpu.CompilerParams(
            collective_id=0, has_side_effects=True, vmem_limit_bytes=36 * 2**20
        ),
    )(*(pltpu.with_memory_space_constraint(value, pltpu.HBM) for value in (merid_coef, cutoffs, polar_flags, zonal_coef, coriolis, layer_weight, adjoint, depth, project, expand, near)))

    return pl.pallas_call(
        final_kernel,
        in_specs=[scalars] + [close] * 2,
        out_specs=pl.BlockSpec(memory_space=pl.ANY),
        out_shape=jax.ShapeDtypeStruct(adjoint.shape, single),
        scratch_shapes=[pltpu.VMEM((2,) + adjoint.shape[1:], single), dma((1 + 2 * level_count // PART,))],
        compiler_params=pltpu.CompilerParams(vmem_limit_bytes=32 * 2**20),
    )(layer_weight, partial, edges)


def plan_for(mesh):
    return on_pair if mesh.shape["lon"] == 2 and mesh.shape["lev"] == 1 else on_device


def solution(mesh):
    return jax.shard_map(
        plan_for(mesh),
        mesh=mesh,
        in_specs=(
            P("member", "lev", "lat", "lon"),
            P("lev", "lat", "lon"),
            P(),
            P(),
            P(),
            P("lev"),
            P(),
            P(),
        ),
        out_specs=P("member", "lev", "lat", "lon"),
        check_vma=False,
    )
```
